512 devices in a mesh: blk: 32 (over z, x_hi), rep: 8 (over y, core), mp: 2 (over x_lo).
Axes of the slice: x: 4 (x_hi: 2, x_lo: 2; x = x_hi * 2 + x_lo), y: 4, z: 16, core: 2. Of those that a mesh axis runs over, the one named last changes fastest.
Arguments:
- x_in: bfloat16 [10240, 256], P('blk'), may hold values from -6 to 6
- weight: bfloat16 [256, 256], replicated, may hold values from -0.375 to 0.375
- out_grad: bfloat16 [16384, 256], P('blk'), may hold values from -6 to 6
- adj_vals: bfloat16 [32, 32, 10, 128, 128], P('blk', 'rep', 'mp'), may hold values from -0.15625 to 0.15625
- adj_tiles: int32 [32, 32, 10, 2], P('blk', 'rep', 'mp'), may hold values from 0 to 3, as said below
- adj_mask: int32 [32, 32, 10], P('blk', 'rep', 'mp'), may hold values from 0 to 1, as said below
- send_rows: int32 [32, 32, 16], P('blk'), may hold values from 0 to 319, as said below
- send_counts: int32 [32, 32], replicated, may hold values from 0 to 16, as said below
Outputs:
- hidden: bfloat16 [16384, 256], P('blk')
- weight_grad: float32 [256, 256], replicated
- input_grad: float32 [10240, 256], P('blk')
The draws below stay inside these ranges and needn't reach their ends.
Inputs may be any that keep to these rules, and one draw needn't show every extreme that they name: For input partition i, the entries send_rows[i, c, s] with s < send_counts[i, c] name every local row 0 to 319 exactly once over all c and s; the other entries are 0. `send_counts`: each row sums to 320; in every draw one owner receives 16 rows from every input partition. `adj_tiles`: within one block pair the 10 tile slots name distinct tile positions. `adj_mask`: every tile slot of offset 0 holds a nonzero tile.
All inputs are finite; a program needn't handle non-finite values.
Results may differ from the reference program's by a relative error of at most 0.005.
Values may be sent and summed in bfloat16 or wider, within the bound.
A program may use at most 64 MiB of HBM per device.

```python
import math
import jax
import jax.numpy as jnp
from jax import lax

F = 256
FO = 256
TILE = 128
ROWS_BLK = 512
NT = 10
SLOTS = 16
IN_ROWS = 320
NODES_PAD = 16384
NODES_IN = 10240
N_BLK = 32


def routing_table(key):
    slot_total = N_BLK * SLOTS
    owner_key, pick_key, shuffle_key = jax.random.split(key, 3)
    full_owner = jax.random.randint(owner_key, (), 0, N_BLK)
    pick_keys = jax.random.split(pick_key, N_BLK)
    shuffle_keys = jax.random.split(shuffle_key, N_BLK)
    owner_of = jnp.arange(slot_total, dtype=jnp.int32) // SLOTS
    slot_of = jnp.arange(slot_total, dtype=jnp.int32) % SLOTS

    def one_source(choose_key, order_key):
        ranking = jax.random.permutation(choose_key, slot_total).astype(jnp.int32)
        ranking = jnp.where(owner_of == full_owner, ranking - slot_total, ranking)
        ordering = jnp.argsort(ranking, stable=True)
        taken = jnp.zeros((slot_total,), jnp.int32).at[ordering[:IN_ROWS]].set(1)
        counts = jnp.sum(taken.reshape(N_BLK, SLOTS), axis=1)
        live_slots = (slot_of.reshape(N_BLK, SLOTS) < counts[:, None]).astype(jnp.int32).reshape(-1)
        position = jnp.cumsum(live_slots) - 1
        shuffle = jax.random.permutation(order_key, IN_ROWS).astype(jnp.int32)
        local_rows = shuffle[jnp.clip(position, 0, IN_ROWS - 1)] * live_slots
        return (local_rows.reshape(N_BLK, SLOTS), counts.astype(jnp.int32))
    return jax.vmap(one_source)(pick_keys, shuffle_keys)


def draw_send_rows(key, part):
    table = routing_table(key)
    return table[0]


def draw_send_counts(key, part):
    table = routing_table(key)
    return table[1]


def draw_adj_tiles(key, part):
    key = jax.random.fold_in(key, 11)
    tiles_dim = ROWS_BLK // TILE
    pair_keys = jax.random.split(key, N_BLK * N_BLK)

    def one_pair(pair_key):
        positions = jax.random.permutation(pair_key, tiles_dim * tiles_dim)[:NT].astype(jnp.int32)
        return jnp.stack([positions // tiles_dim, positions % tiles_dim], axis=-1)
    return jax.vmap(one_pair)(pair_keys).reshape(N_BLK, N_BLK, NT, 2)


def draw_adj_mask(key, part):
    key = jax.random.fold_in(key, 23)
    rank_key, left_key, right_key = jax.random.split(key, 3)
    pair_keys = jax.random.split(rank_key, N_BLK * N_BLK)

    def one_rank(pair_key):
        return jax.random.permutation(pair_key, NT).astype(jnp.int32)
    ranks = jax.vmap(one_rank)(pair_keys).reshape(N_BLK, N_BLK, NT)
    first_draw = jax.random.randint(left_key, (N_BLK, N_BLK), 0, NT + 1)
    second_draw = jax.random.randint(right_key, (N_BLK, N_BLK), 0, NT + 1)
    used = first_draw * second_draw // NT
    offset_ids = lax.broadcasted_iota(jnp.int32, (N_BLK, N_BLK), 1)
    used = jnp.where(offset_ids == 0, NT, used)
    return (ranks < used[:, :, None]).astype(jnp.int32)


def shard_levels(key, extent, cuts, low, largest):
    loudness = 1.0
    for axis_at, shards_of in cuts:
        steps = jax.random.uniform(jax.random.fold_in(jax.random.fold_in(key, 6), axis_at), (shards_of,), jnp.float32, low / len(cuts), largest / len(cuts))
        loudness = loudness * jnp.repeat(jnp.exp(steps), extent[axis_at] // shards_of).reshape((-1,) + (1,) * (len(extent) - 1 - axis_at))
    return loudness


def gaussian(own_key, dims, scale, reach, cuts=(), held_as=jnp.bfloat16):
    loudness = shard_levels(own_key, dims, cuts, -0.22, 0.18) if cuts else 1.0
    result = jax.random.normal(own_key, dims, jnp.float32) * scale * loudness
    return jnp.minimum(jnp.maximum(result, -reach), reach).astype(held_as)


def setup_inputs(seed: int = 0) -> dict:
    streams_of = jax.random.split(jax.random.key(seed), 9)
    x_in = gaussian(streams_of[0], (NODES_IN, F), 1.0, 6.0, ((0, 32),))
    weight = gaussian(streams_of[1], (F, FO), F ** -0.5, 0.375)
    out_grad = gaussian(streams_of[2], (NODES_PAD, FO), 1.0, 6.0, ((0, 32),))
    adj_vals = gaussian(streams_of[3], (N_BLK, N_BLK, NT, TILE, TILE), (N_BLK * ROWS_BLK // 10) ** -0.5, 0.15625, ((0, 32), (1, 8), (2, 2)))
    adj_tiles = draw_adj_tiles(jax.random.fold_in(streams_of[8], 71), 0)
    adj_mask = draw_adj_mask(jax.random.fold_in(streams_of[8], 71), 0)
    send_rows = draw_send_rows(jax.random.fold_in(streams_of[8], 71), 0)
    send_counts = draw_send_counts(jax.random.fold_in(streams_of[8], 71), 0)
    return {"x_in": x_in, "weight": weight, "out_grad": out_grad, "adj_vals": adj_vals, "adj_tiles": adj_tiles, "adj_mask": adj_mask, "send_rows": send_rows, "send_counts": send_counts}


def pick_rows(source_block, row_index):
    return source_block[row_index]

def owner_layout(x_in, send_rows, send_counts):
    slot_ids = jnp.arange(SLOTS, dtype=jnp.int32)
    live_send = slot_ids[None, None, :] < send_counts[:, :, None]
    sources = x_in.reshape(N_BLK, IN_ROWS, F)
    picked = jax.vmap(pick_rows)(sources, send_rows)
    owned = jnp.where(live_send[:, :, :, None], picked, jnp.zeros((), jnp.bfloat16))
    owned = jnp.transpose(owned, (1, 0, 2, 3)).reshape(NODES_PAD, F)
    live_rows = jnp.transpose(live_send, (1, 0, 2)).reshape(NODES_PAD)
    return (owned, live_rows, live_send)

def reference(x_in, weight, out_grad, adj_vals, adj_tiles, adj_mask, send_rows, send_counts):
    tiles_dim = ROWS_BLK // TILE
    owned, live_rows, live_send = owner_layout(x_in, send_rows, send_counts)
    feature_tiles = owned.reshape(N_BLK * tiles_dim, TILE, F)
    offsets = jnp.arange(N_BLK, dtype=jnp.int32)

    def pair_tables(row_block):
        columns = (row_block - offsets) % N_BLK
        source = (columns[:, None] * tiles_dim + adj_tiles[row_block, :, :, 1]).reshape(-1).astype(jnp.int32)
        target = adj_tiles[row_block, :, :, 0].reshape(-1).astype(jnp.int32)
        used = adj_mask[row_block].reshape(-1).astype(jnp.float32)
        values = adj_vals[row_block].reshape(N_BLK * NT, TILE, TILE).astype(jnp.float32)
        return (source, target, used, values)

    def aggregate_block(row_block):
        source, target, used, values = pair_tables(row_block)
        gathered = feature_tiles[source].astype(jnp.float32)
        products = jnp.einsum('nij,njf->nif', values, gathered, precision=lax.Precision.HIGHEST)
        products = products * used[:, None, None]
        summed = jax.ops.segment_sum(products, target, num_segments=tiles_dim)
        return summed.reshape(ROWS_BLK, F)
    aggregated = lax.map(aggregate_block, offsets).reshape(NODES_PAD, F)
    preact = jnp.dot(aggregated, weight.astype(jnp.float32), precision=lax.Precision.HIGHEST)
    gate_value = jax.nn.sigmoid(preact)
    hidden = jnp.where(live_rows[:, None], preact * gate_value, 0.0).astype(jnp.bfloat16)
    slope = gate_value * (1.0 + preact * (1.0 - gate_value))
    pre_grad = jnp.where(live_rows[:, None], out_grad.astype(jnp.float32) * slope, 0.0).astype(jnp.bfloat16)
    weight_grad = jnp.dot(aggregated.T, pre_grad.astype(jnp.float32), precision=lax.Precision.HIGHEST) * (1.0 / math.sqrt(NODES_PAD))
    agg_grad = jnp.dot(pre_grad, weight.T, preferred_element_type=jnp.float32).astype(jnp.bfloat16)
    grad_tiles = agg_grad.reshape(N_BLK, tiles_dim, TILE, F)

    def spread_block(carry, row_block):
        source, target, used, values = pair_tables(row_block)
        gradients = grad_tiles[row_block][target].astype(jnp.float32)
        products = jnp.einsum('nij,nif->njf', values, gradients, precision=lax.Precision.HIGHEST)
        products = products * used[:, None, None]
        carry = carry + jax.ops.segment_sum(products, source, num_segments=N_BLK * tiles_dim)
        return (carry, None)
    start = jnp.zeros((N_BLK * tiles_dim, TILE, F), jnp.float32)
    owned_grad = lax.scan(spread_block, start, offsets)[0]
    owned_grad = owned_grad.reshape(N_BLK, N_BLK, SLOTS, F)
    by_source = jnp.transpose(owned_grad, (1, 0, 2, 3))
    by_source = jnp.where(live_send[:, :, :, None], by_source, 0.0)
    destination = (jnp.arange(N_BLK, dtype=jnp.int32)[:, None, None] * IN_ROWS + send_rows).reshape(-1).astype(jnp.int32)
    input_grad = jnp.zeros((NODES_IN, F), jnp.float32).at[destination].add(by_source.reshape(-1, F))
    return (hidden, weight_grad, input_grad)
```

```python
import functools
import math

import jax
import jax.numpy as jnp
from jax import lax
from jax.experimental import pallas as pl
from jax.experimental.pallas import tpu as pltpu
from jax.sharding import PartitionSpec as P

MESH = pl.DeviceIdType.MESH
BF = jnp.bfloat16
F32 = jnp.float32


def dot(a, b, dims=((1,), (0,))):
    return lax.dot_general(a, b, (dims, ((), ())), preferred_element_type=F32)


def send(src, dst, ssem, rsem, **where):
    pltpu.make_async_remote_copy(
        src_ref=src,
        dst_ref=dst,
        send_sem=ssem,
        recv_sem=rsem,
        device_id=where,
        device_id_type=MESH,
    ).start()


def drain(ref, sem):
    pltpu.make_async_copy(ref, ref, sem).wait()


def kernel(
    keys_ref,
    x_ref,
    w_ref,
    og_ref,
    rowc_ref,
    rowr_ref,
    live_ref,
    keyv_ref,
    adj_ref,
    hid_ref,
    wg_ref,
    ig_ref,
    v0, v1, v2, v3,
    kpv, kps,
    dense, denset,
    outg, fbuf, zbuf,
    r1s, r1r, agg,
    pg, gb,
    bs, br, pown, qb, ar, gg,
    wprod, wa, war, wb, wbr, wc, wd,
    loc_sem, adj_ss, adj_rs, key_ss, key_rs, key_ls,
    ss, rs,
):
    vall = (v0, v1, v2, v3)
    b = lax.axis_index("blk")
    r = lax.axis_index("rep")
    m = lax.axis_index("mp")
    s = 2 * lax.rem(r, 2)
    k = m * 8 + r
    quad = lax.rem(b, 4)
    F1, Z, R1, R2, ZB, A2, SELF, G, WA, WB, WC, WD = range(12)

    def in_group(d):
        t = lax.rem(r * 2 + m + d, 16)
        return t // 2, lax.rem(t, 2)

    barrier = pltpu.get_barrier_semaphore()

    def greet_blk(d, _):
        pl.semaphore_signal(
            barrier, inc=1, device_id={"blk": lax.rem(b + d, 32)}, device_id_type=MESH
        )
        return 0

    lax.fori_loop(1, 32, greet_blk, 0)

    def greet_group(d, _):
        tr, tm = in_group(d)
        pl.semaphore_signal(barrier, inc=1, device_id={"rep": tr, "mp": tm}, device_id_type=MESH)
        return 0

    lax.fori_loop(1, 16, greet_group, 0)

    for p in range(4):
        j = lax.rem(s + p, 4)
        pltpu.make_async_copy(adj_ref.at[j], vall[p].at[pl.ds(0, 5)], loc_sem.at[p]).start()
        vall[p][10] = jnp.zeros((128, 128), BF)

    pick = (rowc_ref[...] == lax.broadcasted_iota(jnp.int32, (512, 320), 1)).astype(BF)
    half = pl.ds(pl.multiple_of(m * 128, 128), 128)
    picked = dot(pick, x_ref[:, half]).astype(BF).reshape(32, 16, 128)
    outg[pl.ds(1, 32)] = picked
    outg[0] = picked[31]

    pl.semaphore_wait(barrier, 46)

    send(keyv_ref, kpv, key_ss, key_rs, mp=1 - m)

    def deliver(d, _):
        t = lax.rem(b + d, 32)
        c = lax.rem(t - 4 * r - s + 64, 32)
        send(outg.at[pl.ds(c, 2)], fbuf.at[b], ss.at[F1], rs.at[F1], blk=t)
        return 0

    lax.fori_loop(1, 32, deliver, 0)
    for p in range(4):
        j = lax.rem(s + p, 4)
        send(adj_ref.at[j], vall[p].at[pl.ds(5, 5)], adj_ss.at[p], adj_rs.at[p], mp=1 - m)
    c_own = lax.rem(b - 4 * r - s + 64, 32)
    fbuf[b] = outg[pl.ds(c_own, 2)]

    drain(kpv, key_rs)
    to_smem = pltpu.make_async_copy(kpv, kps, key_ls)
    to_smem.start()
    to_smem.wait()

    for p in range(4):
        j = lax.rem(s + p, 4)
        pltpu.make_async_copy(adj_ref.at[j], vall[p].at[pl.ds(0, 5)], loc_sem.at[p]).wait()
        drain(vall[p].at[pl.ds(5, 5)], adj_rs.at[p])
        own = [keys_ref[j, t] for t in range(5)]
        other = [kps[j, t] for t in range(5)]
        for row in range(4):
            for col in range(4):
                at = jnp.int32(10)
                for t in range(5):
                    at = jnp.where(own[t] == row * 4 + col, t, at)
                    at = jnp.where(other[t] == row * 4 + col, 5 + t, at)
                tile = vall[p][at]
                dense[p, row * 128:(row + 1) * 128, col * 128:(col + 1) * 128] = tile
                denset[p, col * 128:(col + 1) * 128, row * 128:(row + 1) * 128] = tile.T

    drain(fbuf.at[pl.ds(0, 31)], rs.at[F1])
    t = lax.rem(b + 2 - 2 * s + 32, 32)
    send(fbuf, zbuf, ss.at[Z], rs.at[Z], blk=t)
    part = dot(dense[0], fbuf[:, 1].reshape(512, 128))
    part += dot(dense[1], fbuf[:, 0].reshape(512, 128))
    drain(zbuf, rs.at[Z])
    part += dot(dense[2], zbuf[:, 1].reshape(512, 128))
    part += dot(dense[3], zbuf[:, 0].reshape(512, 128))

    r1s[...] = part.astype(BF).reshape(8, 64, 128)
    r1r[r] = r1s[r]

    def scatter(d, _):
        t = lax.rem(r + d, 8)
        send(r1s.at[t], r1r.at[r], ss.at[R1], rs.at[R1], rep=t)
        return 0

    lax.fori_loop(1, 8, scatter, 0)
    drain(r1r.at[pl.ds(0, 7)], rs.at[R1])
    total = r1r[0].astype(F32)
    for i in range(1, 8):
        total += r1r[i].astype(F32)
    agg[k] = total.astype(BF)

    def gather(d, _):
        tr, tm = in_group(d)
        send(agg.at[k], agg.at[k], ss.at[R2], rs.at[R2], rep=tr, mp=tm)
        return 0

    lax.fori_loop(1, 16, gather, 0)
    drain(agg.at[pl.ds(0, 15)], rs.at[R2])

    w_half = w_ref[half, :]
    for q in range(4):
        rows = slice(q * 128, (q + 1) * 128)
        a0 = agg[2 * q:2 * q + 2].reshape(128, 128)
        a1 = agg[8 + 2 * q:10 + 2 * q].reshape(128, 128)
        preact = dot(a0, w_ref[0:128, :]) + dot(a1, w_ref[128:256, :])
        live = live_ref[rows, :] > 0
        gate = jax.nn.sigmoid(preact)
        hid_ref[rows, :] = jnp.where(live, preact * gate, 0.0).astype(BF)
        slope = gate * (1.0 + preact * (1.0 - gate))
        pre = jnp.where(live, og_ref[rows, :].astype(F32) * slope, 0.0).astype(BF)
        pg[rows, :] = pre
        gb[rows, :] = dot(pre, w_half, ((1,), (1,))).astype(BF)

    g = gb[...]
    bs[:, 1] = dot(denset[2], g).astype(BF).reshape(32, 16, 128)
    bs[:, 0] = dot(denset[3], g).astype(BF).reshape(32, 16, 128)
    t = lax.rem(b - 2 + 2 * s + 32, 32)
    send(bs, br, ss.at[ZB], rs.at[ZB], blk=t)

    mine = agg[pl.ds(m * 8, 8)].reshape(512, 128)
    wprod[...] = dot(mine, pg[...], ((0,), (0,))).reshape(8, 16, 256)
    w16 = wprod[r]
    for a in range(2):
        for c in range(2):
            wa[2 * a + c] = w16[a * 8:(a + 1) * 8, c * 128:(c + 1) * 128]
    war[quad] = wa[quad]
    for e in range(1, 4):
        q = lax.rem(quad + e, 4)
        send(wa.at[q], war.at[quad], ss.at[WA], rs.at[WA], blk=b - quad + q)

    pown[1] = dot(denset[0], g)
    pown[0] = dot(denset[1], g)

    drain(war.at[pl.ds(0, 3)], rs.at[WA])
    tile = war[0] + war[1] + war[2] + war[3]
    wb[...] = tile
    eighth = b // 4
    wbr[eighth] = tile
    for e in range(1, 8):
        send(wb, wbr.at[eighth], ss.at[WB], rs.at[WB], blk=lax.rem(b + 4 * e, 32))

    drain(br, rs.at[ZB])
    for q in range(2):
        mixed = pown[q] + br[:, q].reshape(512, 128).astype(F32)
        qb[:, q] = mixed.astype(BF).reshape(32, 16, 128)

    for q in range(2):
        c = lax.rem(b - 4 * r - s + (q - 1) + 64, 32)
        home, slot = c // 4, lax.rem(c, 4)

        @pl.when(home == r)
        def _():
            pltpu.make_async_copy(qb.at[b, q], ar.at[slot, 2 * r + q], rs.at[A2]).start()

        @pl.when(home != r)
        def _():
            send(qb.at[b, q], ar.at[slot, 2 * r + q], ss.at[SELF], rs.at[A2], rep=home)

        def back(d, _):
            i = lax.rem(b + d, 32)
            send(qb.at[i, q], ar.at[slot, 2 * r + q], ss.at[A2], rs.at[A2], blk=i, rep=home)
            return 0

        lax.fori_loop(1, 32, back, 0)

    drain(wbr.at[pl.ds(0, 7)], rs.at[WB])
    tile = wbr[0]
    for i in range(1, 8):
        tile += wbr[i]
    wc[quad] = tile
    for e in range(1, 4):
        q = lax.rem(quad + e, 4)
        send(wc.at[quad], wc.at[quad], ss.at[WC], rs.at[WC], blk=b - quad + q)
    drain(wc.at[pl.ds(0, 3)], rs.at[WC])
    wd[k] = wc[...]

    def spread_w(d, _):
        tr, tm = in_group(d)
        send(wd.at[k], wd.at[k], ss.at[WD], rs.at[WD], rep=tr, mp=tm)
        return 0

    lax.fori_loop(1, 16, spread_w, 0)

    drain(ar, rs.at[A2])
    total = ar[:, 0].astype(F32)
    for i in range(1, 16):
        total += ar[:, i].astype(F32)
    gg[k] = total.reshape(64, 128).astype(BF)

    def share(d, _):
        tr, tm = in_group(d)
        send(gg.at[k], gg.at[k], ss.at[G], rs.at[G], rep=tr, mp=tm)
        return 0

    lax.fori_loop(1, 16, share, 0)

    drain(wd.at[pl.ds(0, 15)], rs.at[WD])
    for i in range(16):
        for a in range(2):
            for c in range(2):
                wg_ref[i * 16 + a * 8:i * 16 + a * 8 + 8, c * 128:(c + 1) * 128] = (
                    wd[i, 2 * a + c] * (1.0 / 128.0)
                )

    place = (rowr_ref[...] == lax.broadcasted_iota(jnp.int32, (320, 512), 0)).astype(BF)
    drain(gg.at[pl.ds(0, 15)], rs.at[G])
    for h in range(2):
        ig_ref[:, h * 128:(h + 1) * 128] = dot(place, gg[8 * h:8 * h + 8].reshape(512, 128))

    drain(keyv_ref, key_ss)
    for p in range(4):
        drain(vall[p].at[pl.ds(5, 5)], adj_ss.at[p])
    drain(fbuf.at[pl.ds(0, 31)], ss.at[F1])
    drain(fbuf, ss.at[Z])
    drain(r1r.at[pl.ds(0, 7)], ss.at[R1])
    drain(agg.at[pl.ds(0, 15)], ss.at[R2])
    drain(bs, ss.at[ZB])
    drain(qb.at[pl.ds(0, 31)], ss.at[A2])
    for q in range(2):
        c = lax.rem(b - 4 * r - s + (q - 1) + 64, 32)

        @pl.when(c // 4 != r)
        def _():
            drain(qb.at[b, q], ss.at[SELF])

    drain(gg.at[pl.ds(0, 15)], ss.at[G])
    drain(wa.at[pl.ds(0, 3)], ss.at[WA])
    drain(wbr.at[pl.ds(0, 7)], ss.at[WB])
    drain(wc.at[pl.ds(0, 3)], ss.at[WC])
    drain(wd.at[pl.ds(0, 15)], ss.at[WD])


def shards(x_in, weight, out_grad, adj_vals, adj_tiles, adj_mask, send_rows, send_counts):
    my_block = lax.axis_index("blk")
    slot_ids = lax.broadcasted_iota(jnp.int32, (32, 16), 1)
    sent = lax.dynamic_index_in_dim(send_counts, my_block, 0, keepdims=False)
    held = lax.dynamic_index_in_dim(send_counts, my_block, 1, keepdims=False)
    rows = jnp.where(slot_ids < sent[:, None], send_rows[0], -1).reshape(512)
    live = (slot_ids < held[:, None]).astype(F32).reshape(512, 1)
    keys = jnp.where(adj_mask[0] == 1, adj_tiles[0, :, :, 0] * 4 + adj_tiles[0, :, :, 1], 16)
    keys = jnp.pad(keys, ((0, 4), (0, 123)), constant_values=16)

    vmem = pl.BlockSpec(memory_space=pltpu.VMEM)
    V = pltpu.VMEM
    dma = pltpu.SemaphoreType.DMA
    return tuple(
        pl.pallas_call(
            kernel,
            out_shape=(
                jax.ShapeDtypeStruct((512, 256), BF),
                jax.ShapeDtypeStruct((256, 256), F32),
                jax.ShapeDtypeStruct((320, 256), F32),
            ),
            in_specs=[pl.BlockSpec(memory_space=pltpu.SMEM)]
            + [vmem] * 7
            + [pl.BlockSpec(memory_space=pl.ANY)],
            out_specs=(vmem, vmem, vmem),
            scratch_shapes=[V((11, 128, 128), BF)] * 4
            + [
                V((8, 128), jnp.int32),
                pltpu.SMEM((8, 128), jnp.int32),
                V((4, 512, 512), BF),
                V((4, 512, 512), BF),
                V((33, 16, 128), BF),
                V((32, 2, 16, 128), BF),
                V((32, 2, 16, 128), BF),
                V((8, 64, 128), BF),
                V((8, 64, 128), BF),
                V((16, 64, 128), BF),
                V((512, 256), BF),
                V((512, 128), BF),
                V((32, 2, 16, 128), BF),
                V((32, 2, 16, 128), BF),
                V((2, 512, 128), F32),
                V((32, 2, 16, 128), BF),
                V((4, 16, 16, 128), BF),
                V((16, 64, 128), BF),
                V((8, 16, 256), F32),
                V((4, 8, 128), F32),
                V((4, 8, 128), F32),
                V((8, 128), F32),
                V((8, 8, 128), F32),
                V((4, 8, 128), F32),
                V((16, 4, 8, 128), F32),
                dma((4,)),
                dma((4,)),
                dma((4,)),
                dma,
                dma,
                dma,
                dma((12,)),
                dma((12,)),
            ],
            compiler_params=pltpu.CompilerParams(
                collective_id=0, has_side_effects=True, vmem_limit_bytes=40 * 1024 * 1024
            ),
            name="graph_layer",
        )(
            keys,
            x_in,
            weight,
            out_grad,
            rows.reshape(512, 1),
            rows.reshape(1, 512),
            live,
            keys,
            adj_vals[0],
        )
    )


def solution(mesh):
    placed = (
        P("blk", None),
        P(),
        P("blk", None),
        P("blk", "rep", "mp", None, None),
        P("blk", "rep", "mp", None),
        P("blk", "rep", "mp"),
        P("blk", None, None),
        P(),
    )
    return jax.shard_map(
        shards,
        mesh=mesh,
        in_specs=placed,
        out_specs=(P("blk", None), P(), P("blk", None)),
        check_vma=False,
    )
```

```python
import functools

import jax
import jax.numpy as jnp
from jax import lax
from jax.experimental import pallas as pl
from jax.experimental.pallas import tpu as pltpu
from jax.sharding import PartitionSpec as P

MESH = pl.DeviceIdType.MESH
BF = jnp.bfloat16
F32 = jnp.float32


def dot(a, b, dims=((1,), (0,))):
    return lax.dot_general(a, b, (dims, ((), ())), preferred_element_type=F32)


def send(src, dst, ssem, rsem, **where):
    pltpu.make_async_remote_copy(
        src_ref=src,
        dst_ref=dst,
        send_sem=ssem,
        recv_sem=rsem,
        device_id=where,
        device_id_type=MESH,
    ).start()


def drain(ref, sem):
    pltpu.make_async_copy(ref, ref, sem).wait()


def both_ways(n):
    d = 16 - (n + 1) // 2
    return jnp.where(lax.rem(n, 2) == 0, d, 32 - d)


def kernel(
    tiles_ref,
    mask_ref,
    x_ref,
    w_ref,
    og_ref,
    rows_ref,
    counts_ref,
    adj_ref,
    hid_ref,
    wg_ref,
    ig_ref,
    v0, v1, v2, v3,
    xv, wv, ogv, rowsv, countsv,
    own_ts, own_ms, mp_tv, mp_mv, mp_ts, mp_ms,
    dense, denset,
    outg, fbuf, zbuf,
    r1s, r1r, agg,
    pg, gb,
    bs, br, qb, ar, gg,
    wprod, wa, war, wb, wbr, wc, wd,
    loc_sem, in_sem, adj_ss, adj_rs, key_ss, key_rs, key_ls,
    ss, rs,
):
    vall = (v0, v1, v2, v3)
    b = lax.axis_index("blk")
    r = lax.axis_index("rep")
    m = lax.axis_index("mp")
    s = 2 * lax.rem(r, 2)
    h = lax.rem(m + b, 2)
    k = h * 8 + r
    quad = lax.rem(b, 4)
    F1, Z, R1, R2, ZB, A2, SELF, G, WA, WB, WC, WD = range(0, 24, 2)

    def at_blk(t):
        return {"blk": t, "mp": lax.rem(h + t, 2)}

    def in_group(d):
        t = lax.rem(r * 2 + m + d, 16)
        return t // 2, lax.rem(t, 2)

    barrier = pltpu.get_barrier_semaphore()

    def greet_blk(d, _):
        pl.semaphore_signal(
            barrier, inc=1, device_id=at_blk(lax.rem(b + d, 32)), device_id_type=MESH
        )
        return 0

    lax.fori_loop(1, 32, greet_blk, 0)

    def greet_group(d, _):
        tr, tm = in_group(d)
        pl.semaphore_signal(barrier, inc=1, device_id={"rep": tr, "mp": tm}, device_id_type=MESH)
        return 0

    lax.fori_loop(1, 16, greet_group, 0)

    staged = (
        (rows_ref, rowsv),
        (counts_ref, countsv),
        (x_ref, xv),
        (tiles_ref, own_ts),
        (mask_ref, own_ms),
        (w_ref, wv),
        (og_ref, ogv),
    )
    for i, (src, dst) in enumerate(staged):
        pltpu.make_async_copy(src, dst, in_sem.at[i]).start()

    def arrived(i):
        src, dst = staged[i]
        pltpu.make_async_copy(src, dst, in_sem.at[i]).wait()

    for p in range(4):
        j = lax.rem(s + p, 4)
        pltpu.make_async_copy(adj_ref.at[j], vall[p].at[pl.ds(0, 5)], loc_sem.at[p]).start()
        vall[p][10] = jnp.zeros((128, 128), BF)

    pl.semaphore_wait(barrier, 46)

    send(tiles_ref, mp_tv, key_ss.at[0], key_rs.at[0], mp=1 - m)
    send(mask_ref, mp_mv, key_ss.at[1], key_rs.at[1], mp=1 - m)

    def pass_tiles(p):
        j = lax.rem(s + p, 4)
        send(adj_ref.at[j], vall[p].at[pl.ds(5, 5)], adj_ss.at[p], adj_rs.at[p], mp=1 - m)

    for p in range(4):
        pass_tiles(p)

    iota = functools.partial(lax.broadcasted_iota, jnp.int32)
    expand = (iota((512, 32), 0) // 16 == iota((512, 32), 1)).astype(BF)
    in_slot = lax.rem(iota((512, 16), 0), 16) == iota((512, 16), 1)
    mine = (iota((32, 16), 0) == b).astype(BF)
    arrived(0)
    arrived(1)
    counts = countsv[...].astype(F32).astype(BF)
    sent = dot(mine, counts, ((0,), (0,)))
    row = jnp.where(iota((16, 32), 0).astype(F32) < sent, rowsv[...], 384)
    high = (row // 128).astype(F32).astype(BF)
    low = lax.rem(row, 128).astype(F32).astype(BF)
    full = dot(expand, high, ((1,), (1,))) * 128.0 + dot(expand, low, ((1,), (1,)))
    rowc = jnp.sum(jnp.where(in_slot, full, 0.0), axis=1, keepdims=True)

    pick = (rowc == iota((512, 320), 1).astype(F32)).astype(BF)
    half = pl.ds(pl.multiple_of(h * 128, 128), 128)
    arrived(2)
    picked = dot(pick, xv[:, half]).astype(BF).reshape(32, 16, 128)
    outg[pl.ds(1, 32)] = picked
    outg[0] = picked[31]

    def deliver(n, _):
        t = lax.rem(b + both_ways(n), 32)
        c = lax.rem(t - 4 * r - s + 64, 32)
        send(outg.at[pl.ds(c, 2)], fbuf.at[b], ss.at[F1], rs.at[F1], **at_blk(t))
        return 0

    lax.fori_loop(0, 31, deliver, 0)
    c_own = lax.rem(b - 4 * r - s + 64, 32)
    fbuf[b] = outg[pl.ds(c_own, 2)]

    held = dot(counts, mine)
    alive = dot(expand, (iota((32, 16), 1).astype(F32) < held).astype(BF))
    live = jnp.sum(jnp.where(in_slot, alive, 0.0), axis=1, keepdims=True) > 0.5
    expand_t = (iota((32, 512), 1) // 16 == iota((32, 512), 0)).astype(BF)
    in_slot_t = lax.rem(iota((16, 512), 1), 16) == iota((16, 512), 0)
    full_t = dot(high, expand_t) * 128.0 + dot(low, expand_t)
    rowr = jnp.sum(jnp.where(in_slot_t, full_t, 0.0), axis=0, keepdims=True)

    arrived(3)
    arrived(4)
    drain(mp_tv, key_rs.at[0])
    drain(mp_mv, key_rs.at[1])
    for i, (src, dst) in enumerate(((mp_tv, mp_ts), (mp_mv, mp_ms))):
        pltpu.make_async_copy(src, dst, key_ls.at[i]).start()
    for i, (src, dst) in enumerate(((mp_tv, mp_ts), (mp_mv, mp_ms))):
        pltpu.make_async_copy(src, dst, key_ls.at[i]).wait()

    def build(p):
        j = lax.rem(s + p, 4)
        pltpu.make_async_copy(adj_ref.at[j], vall[p].at[pl.ds(0, 5)], loc_sem.at[p]).wait()
        drain(vall[p].at[pl.ds(5, 5)], adj_rs.at[p])

        def places(ts, ms):
            return [
                jnp.where(ms[j, t] == 1, ts[j, 0, t] * 4 + ts[j, 1, t], 16) for t in range(5)
            ]

        own, other = places(own_ts, own_ms), places(mp_ts, mp_ms)
        for row in range(4):
            for col in range(4):
                at = jnp.int32(10)
                for t in range(5):
                    at = jnp.where(own[t] == row * 4 + col, t, at)
                    at = jnp.where(other[t] == row * 4 + col, 5 + t, at)
                tile = vall[p][at]
                dense[p, row * 128:(row + 1) * 128, col * 128:(col + 1) * 128] = tile

    def transpose(p):
        for row in range(4):
            for col in range(4):
                tile = dense[p, row * 128:(row + 1) * 128, col * 128:(col + 1) * 128]
                denset[p, col * 128:(col + 1) * 128, row * 128:(row + 1) * 128] = tile.T

    for p in range(3):
        build(p)

    drain(fbuf.at[pl.ds(0, 31)], rs.at[F1])
    t = lax.rem(b + 2 - 2 * s + 32, 32)
    send(fbuf, zbuf, ss.at[Z], rs.at[Z], **at_blk(t))
    part = dot(dense[0], fbuf[:, 1].reshape(512, 128))
    part += dot(dense[1], fbuf[:, 0].reshape(512, 128))
    build(3)
    drain(zbuf, rs.at[Z])
    part += dot(dense[2], zbuf[:, 1].reshape(512, 128))
    part += dot(dense[3], zbuf[:, 0].reshape(512, 128))

    r1s[...] = part.astype(BF).reshape(8, 64, 128)
    r1r[r] = r1s[r]

    def scatter(d, _):
        t = lax.rem(r + d, 8)
        send(r1s.at[t], r1r.at[r], ss.at[R1], rs.at[R1], rep=t)
        return 0

    lax.fori_loop(1, 8, scatter, 0)
    transpose(2)
    transpose(3)
    drain(r1r.at[pl.ds(0, 7)], rs.at[R1])
    total = r1r[0].astype(F32)
    for i in range(1, 8):
        total += r1r[i].astype(F32)
    agg[k] = total.astype(BF)

    def gather(d, _):
        tr, tm = in_group(d)
        send(agg.at[k], agg.at[k], ss.at[R2], rs.at[R2], rep=tr, mp=tm)
        return 0

    lax.fori_loop(1, 16, gather, 0)
    transpose(0)
    transpose(1)
    drain(agg.at[pl.ds(0, 15)], rs.at[R2])

    arrived(5)
    arrived(6)
    w_half = wv[half, :]
    for q in range(4):
        rows = slice(q * 128, (q + 1) * 128)
        a0 = agg[2 * q:2 * q + 2].reshape(128, 128)
        a1 = agg[8 + 2 * q:10 + 2 * q].reshape(128, 128)
        preact = dot(a0, wv[0:128, :]) + dot(a1, wv[128:256, :])
        gate = jax.nn.sigmoid(preact)
        hid_ref[rows, :] = jnp.where(live[rows], preact * gate, 0.0).astype(BF)
        slope = gate * (1.0 + preact * (1.0 - gate))
        pre = jnp.where(live[rows], ogv[rows, :].astype(F32) * slope, 0.0).astype(BF)
        pg[rows, :] = pre
        gb[rows, :] = dot(pre, w_half, ((1,), (1,))).astype(BF)

    g = gb[...]
    t = lax.rem(b - 2 + 2 * s + 32, 32)
    for q in (1, 0):
        bs[q] = dot(denset[3 - q], g).astype(BF)
        send(bs.at[q], br.at[q], ss.at[ZB + q], rs.at[ZB + q], **at_blk(t))

    wprod[...] = dot(agg[pl.ds(h * 8, 8)].reshape(512, 128), pg[...], ((0,), (0,))).reshape(
        8, 16, 256
    )
    w16 = wprod[r]
    for a in range(2):
        for c in range(2):
            wa[2 * a + c] = w16[a * 8:(a + 1) * 8, c * 128:(c + 1) * 128]
    war[quad] = wa[quad]
    for e in range(1, 4):
        q = lax.rem(quad + e, 4)
        send(wa.at[q], war.at[quad], ss.at[WA], rs.at[WA], **at_blk(b - quad + q))
    eighth = b // 4

    for q in (1, 0):
        own = dot(denset[1 - q], g)
        drain(br.at[q], rs.at[ZB + q])
        qb[q] = (own + br[q].astype(F32)).astype(BF).reshape(32, 16, 128)
        if q == 1:
            drain(war.at[pl.ds(0, 3)], rs.at[WA])
            tile = war[0] + war[1] + war[2] + war[3]
            wb[...] = tile
            wbr[eighth] = tile
            for e in range(1, 8):
                send(wb, wbr.at[eighth], ss.at[WB], rs.at[WB], **at_blk(lax.rem(b + 4 * e, 32)))
        c = lax.rem(b - 4 * r - s + (q - 1) + 64, 32)
        home, slot = c // 4, lax.rem(c, 4)

        @pl.when(home == r)
        def _():
            pltpu.make_async_copy(qb.at[q, b], ar.at[slot, 2 * r + q], rs.at[A2]).start()

        @pl.when(home != r)
        def _():
            send(qb.at[q, b], ar.at[slot, 2 * r + q], ss.at[SELF + q], rs.at[A2], rep=home)

        def back(n, _):
            i = lax.rem(b + both_ways(n), 32)
            send(
                qb.at[q, i],
                ar.at[slot, 2 * r + q],
                ss.at[A2 + q],
                rs.at[A2],
                rep=home,
                **at_blk(i),
            )
            return 0

        lax.fori_loop(0, 31, back, 0)

    drain(wbr.at[pl.ds(0, 7)], rs.at[WB])
    tile = wbr[0]
    for i in range(1, 8):
        tile += wbr[i]
    wc[quad] = tile
    for e in range(1, 4):
        q = lax.rem(quad + e, 4)
        send(wc.at[quad], wc.at[quad], ss.at[WC], rs.at[WC], **at_blk(b - quad + q))
    place = (rowr == iota((320, 512), 0).astype(F32)).astype(BF)
    drain(wc.at[pl.ds(0, 3)], rs.at[WC])
    wd[k] = wc[...]

    def spread_w(d, _):
        tr, tm = in_group(d)
        send(wd.at[k], wd.at[k], ss.at[WD], rs.at[WD], rep=tr, mp=tm)
        return 0

    lax.fori_loop(1, 16, spread_w, 0)

    drain(ar, rs.at[A2])
    total = ar[:, 0].astype(F32)
    for i in range(1, 16):
        total += ar[:, i].astype(F32)
    gg[k] = total.reshape(64, 128).astype(BF)

    def share(d, _):
        tr, tm = in_group(d)
        send(gg.at[k], gg.at[k], ss.at[G], rs.at[G], rep=tr, mp=tm)
        return 0

    lax.fori_loop(1, 16, share, 0)

    drain(wd.at[pl.ds(0, 15)], rs.at[WD])
    for i in range(16):
        for a in range(2):
            for c in range(2):
                wg_ref[i * 16 + a * 8:i * 16 + a * 8 + 8, c * 128:(c + 1) * 128] = (
                    wd[i, 2 * a + c] * (1.0 / 128.0)
                )

    drain(gg.at[pl.ds(0, 15)], rs.at[G])
    for h in range(2):
        ig_ref[:, h * 128:(h + 1) * 128] = dot(place, gg[8 * h:8 * h + 8].reshape(512, 128))


    drain(mp_tv, key_ss.at[0])
    drain(mp_mv, key_ss.at[1])
    for p in range(4):
        drain(vall[p].at[pl.ds(5, 5)], adj_ss.at[p])
    drain(fbuf.at[pl.ds(0, 31)], ss.at[F1])
    drain(fbuf, ss.at[Z])
    drain(r1r.at[pl.ds(0, 7)], ss.at[R1])
    drain(agg.at[pl.ds(0, 15)], ss.at[R2])
    for q in range(2):
        drain(bs.at[q], ss.at[ZB + q])
        drain(qb.at[q, pl.ds(0, 31)], ss.at[A2 + q])
        c = lax.rem(b - 4 * r - s + (q - 1) + 64, 32)

        @pl.when(c // 4 != r)
        def _():
            drain(qb.at[q, b], ss.at[SELF + q])

    drain(gg.at[pl.ds(0, 15)], ss.at[G])
    drain(wa.at[pl.ds(0, 3)], ss.at[WA])
    drain(wbr.at[pl.ds(0, 7)], ss.at[WB])
    drain(wc.at[pl.ds(0, 3)], ss.at[WC])
    drain(wd.at[pl.ds(0, 15)], ss.at[WD])


def hand_over(a0, a1, a2, o0, o1, o2, v0, v1, v2, sem):
    trips = ((a0, v0, o0), (a1, v1, o1), (a2, v2, o2))
    for i, (src, mid, _) in enumerate(trips):
        pltpu.make_async_copy(src, mid, sem.at[i]).start()
    for i, (src, mid, dst) in enumerate(trips):
        pltpu.make_async_copy(src, mid, sem.at[i]).wait()
        pltpu.make_async_copy(mid, dst, sem.at[3 + i]).start()
    for i, (_, mid, dst) in enumerate(trips):
        pltpu.make_async_copy(mid, dst, sem.at[3 + i]).wait()


def shards(x_in, weight, out_grad, adj_vals, adj_tiles, adj_mask, send_rows, send_counts):
    hbm = pl.BlockSpec(memory_space=pltpu.HBM)
    vmem = pl.BlockSpec(memory_space=pltpu.VMEM)
    V = pltpu.VMEM
    S = pltpu.SMEM
    I32 = jnp.int32
    dma = pltpu.SemaphoreType.DMA
    outs = (
        jax.ShapeDtypeStruct((512, 256), BF),
        jax.ShapeDtypeStruct((256, 256), F32),
        jax.ShapeDtypeStruct((320, 256), F32),
    )
    results = pl.pallas_call(
        kernel,
        out_shape=outs,
        in_specs=[hbm] * 8,
        out_specs=(vmem,) * 3,
        scratch_shapes=[V((11, 128, 128), BF)] * 4
        + [
            V((320, 256), BF),
            V((256, 256), BF),
            V((512, 256), BF),
            V((16, 32), I32),
            V((32, 32), I32),
            S((4, 2, 5), I32),
            S((4, 5), I32),
            V((4, 2, 5), I32),
            V((4, 5), I32),
            S((4, 2, 5), I32),
            S((4, 5), I32),
            V((4, 512, 512), BF),
            V((4, 512, 512), BF),
            V((33, 16, 128), BF),
            V((32, 2, 16, 128), BF),
            V((32, 2, 16, 128), BF),
            V((8, 64, 128), BF),
            V((8, 64, 128), BF),
            V((16, 64, 128), BF),
            V((512, 256), BF),
            V((512, 128), BF),
            V((2, 512, 128), BF),
            V((2, 512, 128), BF),
            V((2, 32, 16, 128), BF),
            V((4, 16, 16, 128), BF),
            V((16, 64, 128), BF),
            V((8, 16, 256), F32),
            V((4, 8, 128), F32),
            V((4, 8, 128), F32),
            V((8, 128), F32),
            V((8, 8, 128), F32),
            V((4, 8, 128), F32),
            V((16, 4, 8, 128), F32),
            dma((4,)),
            dma((7,)),
            dma((4,)),
            dma((4,)),
            dma((2,)),
            dma((2,)),
            dma((2,)),
            dma((24,)),
            dma((24,)),
        ],
        compiler_params=pltpu.CompilerParams(
            collective_id=0, has_side_effects=True, vmem_limit_bytes=62 * 1024 * 1024
        ),
        name="graph_layer",
    )(
        jnp.swapaxes(adj_tiles[0], 1, 2),
        adj_mask[0],
        x_in,
        weight,
        out_grad,
        send_rows[0].T,
        send_counts,
        adj_vals[0],
    )
    return pl.pallas_call(
        hand_over,
        out_shape=outs,
        in_specs=[pl.BlockSpec(memory_space=pl.ANY)] * 3,
        out_specs=(hbm,) * 3,
        scratch_shapes=[V(o.shape, o.dtype) for o in outs] + [dma((6,))],
        compiler_params=pltpu.CompilerParams(vmem_limit_bytes=62 * 1024 * 1024),
        name="hand_over",
    )(*results)


def solution(mesh):
    placed = (
        P("blk", None),
        P(),
        P("blk", None),
        P("blk", "rep", "mp", None, None),
        P("blk", "rep", "mp", None),
        P("blk", "rep", "mp"),
        P("blk", None, None),
        P(),
    )
    return jax.shard_map(
        shards,
        mesh=mesh,
        in_specs=placed,
        out_specs=(P("blk", None), P(), P("blk", None)),
        check_vma=False,
    )
```

```python
import functools

import jax
import jax.numpy as jnp
from jax import lax
from jax.experimental import pallas as pl
from jax.experimental.pallas import tpu as pltpu
from jax.sharding import PartitionSpec as P

MESH = pl.DeviceIdType.MESH
BF = jnp.bfloat16
F32 = jnp.float32


def dot(a, b, dims=((1,), (0,))):
    return lax.dot_general(a, b, (dims, ((), ())), preferred_element_type=F32)


def send(src, dst, ssem, rsem, **where):
    pltpu.make_async_remote_copy(
        src_ref=src,
        dst_ref=dst,
        send_sem=ssem,
        recv_sem=rsem,
        device_id=where,
        device_id_type=MESH,
    ).start()


def drain(ref, sem):
    pltpu.make_async_copy(ref, ref, sem).wait()


def kernel(
    tiles_ref,
    mask_ref,
    x_ref,
    w_ref,
    og_ref,
    rows_ref,
    counts_ref,
    adj_ref,
    hid_ref,
    wg_ref,
    ig_ref,
    v0, v1,
    xv, wv, ogv, rowsv, countsv,
    own_ts, own_ms, mp_tv, mp_mv, mp_ts, mp_ms,
    dense, denset,
    outg, fq, fr, nat,
    r1s, r1r, agg,
    pg, gb,
    pb, xr, mb, ar, gg,
    wprod, wa, war, wb, wbr, wc, wd,
    hidv, wgv, igv,
    loc_sem, in_sem, out_sem, adj_ss, adj_rs, key_ss, key_rs, key_ls,
    ss, rs,
):
    vall = (v0, v1)
    b = lax.axis_index("blk")
    r = lax.axis_index("rep")
    m = lax.axis_index("mp")
    z = b // 2
    parity = lax.rem(b, 2)
    h = lax.rem(m + b, 2)
    k = r * 2 + m
    kw = r * 2 + h
    quad = lax.rem(b, 4)
    R1, R2, G, WA, WB, WC, WD, A2 = range(8)
    F1, XF, XB, A2S, SELF = 8, 10, 12, 14, 16

    def at_blk(t):
        return {"blk": t, "mp": lax.rem(h + t, 2)}

    def in_group(d):
        t = lax.rem(k + d, 16)
        return t // 2, lax.rem(t, 2)

    barrier = pltpu.get_barrier_semaphore()

    def greet(where):
        pl.semaphore_signal(barrier, inc=1, device_id=where, device_id_type=MESH)

    greet({"blk": lax.rem(b + 16, 32)})

    def greet_z(n, _):
        greet({"blk": lax.rem(b + 14 - 2 * n, 32)})
        greet({"blk": lax.rem(b + 18 + 2 * n, 32)})
        return 0

    lax.fori_loop(0, 7, greet_z, 0)

    def greet_group(d, _):
        tr, tm = in_group(d)
        greet({"rep": tr, "mp": tm})
        return 0

    lax.fori_loop(1, 16, greet_group, 0)
    for d in (29, 3, 31, 1):
        greet(at_blk(lax.rem(b + d, 32)))

    staged = (
        (rows_ref, rowsv),
        (counts_ref, countsv),
        (x_ref, xv),
        (tiles_ref, own_ts),
        (mask_ref, own_ms),
        (w_ref, wv),
        (og_ref, ogv),
    )
    for i, (src, dst) in enumerate(staged):
        pltpu.make_async_copy(src, dst, in_sem.at[i]).start()

    def arrived(i):
        src, dst = staged[i]
        pltpu.make_async_copy(src, dst, in_sem.at[i]).wait()

    for p in range(2):
        pltpu.make_async_copy(
            adj_ref.at[m + 2 * p], vall[p].at[pl.ds(0, 5)], loc_sem.at[p]
        ).start()
        vall[p][10] = jnp.zeros((128, 128), BF)

    pl.semaphore_wait(barrier, 34)

    send(tiles_ref, mp_tv, key_ss.at[0], key_rs.at[0], mp=1 - m)
    send(mask_ref, mp_mv, key_ss.at[1], key_rs.at[1], mp=1 - m)
    for p in range(2):
        send(
            adj_ref.at[1 - m + 2 * p],
            vall[p].at[pl.ds(5, 5)],
            adj_ss.at[p],
            adj_rs.at[p],
            mp=1 - m,
        )

    iota = functools.partial(lax.broadcasted_iota, jnp.int32)
    expand = (2 * (iota((256, 32), 0) // 16) + h == iota((256, 32), 1)).astype(BF)
    in_slot = lax.rem(iota((256, 16), 0), 16) == iota((256, 16), 1)
    mine = (iota((32, 16), 0) == b).astype(BF)
    arrived(0)
    arrived(1)
    counts = countsv[...].astype(F32).astype(BF)
    sent = dot(mine, counts, ((0,), (0,)))
    row = jnp.where(iota((16, 32), 0).astype(F32) < sent, rowsv[...], 384)
    high = (row // 128).astype(F32).astype(BF)
    low = lax.rem(row, 128).astype(F32).astype(BF)
    full = dot(expand, high, ((1,), (1,))) * 128.0 + dot(expand, low, ((1,), (1,)))
    rowc = jnp.sum(jnp.where(in_slot, full, 0.0), axis=1, keepdims=True)
    pick = (rowc == iota((256, 320), 1).astype(F32)).astype(BF)
    arrived(2)
    outg[...] = dot(pick, xv[...]).astype(BF).reshape(16, 16, 256)

    def owner_at(d):
        return lax.rem(2 * lax.rem(z + d, 16) + parity - 4 * r - m + 64, 32) // 2

    def deliver(n, _):
        up = 7 - n
        send(
            outg.at[owner_at(up)],
            fq.at[0, n],
            ss.at[F1],
            rs.at[F1],
            blk=lax.rem(b + 2 * up, 32),
        )
        send(
            outg.at[owner_at(8 + n)],
            fq.at[1, 7 - n],
            ss.at[F1 + 1],
            rs.at[F1 + 1],
            blk=lax.rem(b + 2 * (9 + n), 32),
        )
        return 0

    lax.fori_loop(0, 7, deliver, 0)
    fq[0, 7] = outg[owner_at(0)]
    fq[1, 0] = outg[owner_at(15)]

    def first_z(t, j):
        return lax.rem(t // 2 + (9 if j < 2 else 0), 16)

    held = dot(counts, mine)
    expand_r = (iota((512, 32), 0) // 16 == iota((512, 32), 1)).astype(BF)
    in_slot_r = lax.rem(iota((512, 16), 0), 16) == iota((512, 16), 1)
    alive = dot(expand_r, (iota((32, 16), 1).astype(F32) < held).astype(BF))
    live = jnp.sum(jnp.where(in_slot_r, alive, 0.0), axis=1, keepdims=True) > 0.5
    at = iota((32, 512), 1)
    owner = 4 * (at // 64) + 2 * lax.rem(at // 16, 2) + lax.rem(at // 32, 2)
    expand_t = (owner == iota((32, 512), 0)).astype(BF)
    in_slot_t = lax.rem(iota((16, 512), 1), 16) == iota((16, 512), 0)
    full_t = dot(high, expand_t) * 128.0 + dot(low, expand_t)
    rowr = jnp.sum(jnp.where(in_slot_t, full_t, 0.0), axis=0, keepdims=True)

    arrived(3)
    arrived(4)
    drain(mp_tv, key_rs.at[0])
    drain(mp_mv, key_rs.at[1])
    for i, (src, dst) in enumerate(((mp_tv, mp_ts), (mp_mv, mp_ms))):
        pltpu.make_async_copy(src, dst, key_ls.at[i]).start()
    for i, (src, dst) in enumerate(((mp_tv, mp_ts), (mp_mv, mp_ms))):
        pltpu.make_async_copy(src, dst, key_ls.at[i]).wait()

    def build(p):
        j = m + 2 * p
        pltpu.make_async_copy(
            adj_ref.at[m + 2 * p], vall[p].at[pl.ds(0, 5)], loc_sem.at[p]
        ).wait()
        drain(vall[p].at[pl.ds(5, 5)], adj_rs.at[p])

        def places(ts, ms):
            return [
                jnp.where(ms[j, t] == 1, ts[j, 0, t] * 4 + ts[j, 1, t], 16) for t in range(5)
            ]

        own, other = places(own_ts, own_ms), places(mp_ts, mp_ms)
        for row in range(4):
            for col in range(4):
                at = jnp.int32(10)
                for t in range(5):
                    at = jnp.where(own[t] == row * 4 + col, t, at)
                    at = jnp.where(other[t] == row * 4 + col, 5 + t, at)
                tile = vall[p][at]
                dense[p, row * 128:(row + 1) * 128, col * 128:(col + 1) * 128] = tile

    def transpose(p):
        for row in range(4):
            for col in range(4):
                tile = dense[p, row * 128:(row + 1) * 128, col * 128:(col + 1) * 128]
                denset[p, col * 128:(col + 1) * 128, row * 128:(row + 1) * 128] = tile.T

    def others(p):
        for e in range(1, 4):
            to = lax.rem(m + 2 * p + e, 4)
            yield to, lax.rem(b - m - 2 * p + to + 32, 32)

    build(0)
    for p in range(2):
        drain(fq.at[p, pl.ds(0, 7)], rs.at[F1 + p])
        for to, t in others(p):
            send(
                fq.at[p],
                fr.at[to // 2, m + 2 * p],
                ss.at[XF + p],
                rs.at[XF + to // 2],
                **at_blk(t),
            )
        fr[p, m + 2 * p] = fq[p]
    build(1)

    part = None
    for p in range(2):
        drain(fr.at[p, pl.ds(0, 3)], rs.at[XF + p])
        for j in range(4):
            t = lax.rem(b - m - 2 * p + j + 32, 32)
            for n in range(8):
                nat[p, lax.rem(first_z(t, j) + n, 16), lax.rem(t, 2)] = fr[p, j, n]
        term = dot(dense[p], nat[p].reshape(512, 256))
        part = term if part is None else part + term

    r1s[...] = part.astype(BF).reshape(16, 32, 256)

    def scatter(d, _):
        tr, tm = in_group(d)
        send(r1s.at[2 * tr + tm], r1r.at[k], ss.at[R1], rs.at[R1], rep=tr, mp=tm)
        return 0

    lax.fori_loop(1, 16, scatter, 0)
    r1r[k] = r1s[k]
    transpose(0)
    drain(r1r.at[pl.ds(0, 15)], rs.at[R1])
    total = r1r[0].astype(F32)
    for i in range(1, 16):
        total += r1r[i].astype(F32)
    agg[k] = total.astype(BF)

    def gather(d, _):
        tr, tm = in_group(d)
        send(agg.at[k], agg.at[k], ss.at[R2], rs.at[R2], rep=tr, mp=tm)
        return 0

    lax.fori_loop(1, 16, gather, 0)
    transpose(1)
    arrived(5)
    arrived(6)
    drain(agg.at[pl.ds(0, 15)], rs.at[R2])

    for q in range(4):
        rows = slice(q * 128, (q + 1) * 128)
        preact = dot(agg[4 * q:4 * q + 4].reshape(128, 256), wv[...])
        gate = jax.nn.sigmoid(preact)
        hidv[rows, :] = jnp.where(live[rows], preact * gate, 0.0).astype(BF)
        slope = gate * (1.0 + preact * (1.0 - gate))
        pre = jnp.where(live[rows], ogv[rows, :].astype(F32) * slope, 0.0).astype(BF)
        pg[rows, :] = pre
        gb[rows, :] = dot(pre, wv[...], ((1,), (1,))).astype(BF)

    for p in range(2):
        terms = dot(denset[p], gb[...]).astype(BF).reshape(16, 2, 16, 256)
        for q in range(2):
            pb[p, q, 0:16] = terms[:, q]
            pb[p, q, 16:24] = terms[0:8, q]
        for to, t in others(p):
            start = lax.rem(t // 2 + jnp.where(to < 2, 9, 0), 16)
            send(
                pb.at[p, lax.rem(t, 2), pl.ds(start, 8)],
                xr.at[to // 2, m + 2 * p],
                ss.at[XB + p],
                rs.at[XB + to // 2],
                **at_blk(t),
            )
        xr[p, m + 2 * p] = pb[p, parity, pl.ds(first_z(b, 2 * p), 8)]
    pltpu.make_async_copy(hidv, hid_ref, out_sem.at[0]).start()

    columns = pl.ds(pl.multiple_of((r // 4) * 128, 128), 128)
    wprod[...] = dot(agg[:, :, columns].reshape(512, 128), pg[...], ((0,), (0,))).reshape(8, 16, 256)
    w16 = wprod[lax.rem(r, 4) * 2 + h]
    for a in range(2):
        for c in range(2):
            wa[2 * a + c] = w16[a * 8:(a + 1) * 8, c * 128:(c + 1) * 128]
    war[quad] = wa[quad]
    for e in range(1, 4):
        q = lax.rem(quad + e, 4)
        send(wa.at[q], war.at[quad], ss.at[WA], rs.at[WA], **at_blk(b - quad + q))
    eighth = b // 4

    for p in range(2):
        drain(xr.at[p, pl.ds(0, 3)], rs.at[XB + p])
        total = xr[p, 0].astype(F32)
        for i in range(1, 4):
            total += xr[p, i].astype(F32)
        mb[p] = total.astype(BF)
        if p == 0:
            drain(war.at[pl.ds(0, 3)], rs.at[WA])
            tile = war[0] + war[1] + war[2] + war[3]
            wb[...] = tile
            wbr[eighth] = tile
            for e in range(1, 8):
                send(wb, wbr.at[eighth], ss.at[WB], rs.at[WB], blk=lax.rem(b + 4 * e, 32))
        c = lax.rem(b - 4 * r - m - 2 * p + 64, 32)
        home, slot = c // 4, lax.rem(c, 4) // 2

        def back(n, _):
            away = 7 - n
            send(
                mb.at[p, n if p == 0 else away],
                ar.at[slot, r],
                ss.at[A2S + p],
                rs.at[A2],
                blk=lax.rem(b + (32 - 2 * away if p == 0 else 2 * away), 32),
                rep=home,
            )
            return 0

        lax.fori_loop(0, 7, back, 0)
        here = 7 if p == 0 else 0

        @pl.when(home == r)
        def _():
            pltpu.make_async_copy(mb.at[p, here], ar.at[slot, r], rs.at[A2]).start()

        @pl.when(home != r)
        def _():
            send(mb.at[p, here], ar.at[slot, r], ss.at[SELF + p], rs.at[A2], rep=home)

    place = (rowr == iota((320, 512), 0).astype(F32)).astype(BF)
    drain(wbr.at[pl.ds(0, 7)], rs.at[WB])
    tile = wbr[0]
    for i in range(1, 8):
        tile += wbr[i]
    wc[quad] = tile
    for e in range(1, 4):
        q = lax.rem(quad + e, 4)
        send(wc.at[quad], wc.at[quad], ss.at[WC], rs.at[WC], **at_blk(b - quad + q))

    drain(ar, rs.at[A2])
    total = ar[:, 0].astype(F32)
    for i in range(1, 8):
        total += ar[:, i].astype(F32)
    gg[kw] = total.astype(BF)

    def share(d, _):
        tr, tm = in_group(d)
        send(gg.at[kw], gg.at[kw], ss.at[G], rs.at[G], rep=tr, mp=tm)
        return 0

    lax.fori_loop(1, 16, share, 0)

    drain(wc.at[pl.ds(0, 3)], rs.at[WC])
    for a in range(2):
        for c in range(2):
            w_part = wc[2 * a + c]
            wprod[0, a * 8:(a + 1) * 8, c * 128:(c + 1) * 128] = w_part
    wd[kw] = wprod[0].astype(BF)

    def spread_w(d, _):
        tr, tm = in_group(d)
        send(wd.at[kw], wd.at[kw], ss.at[WD], rs.at[WD], rep=tr, mp=tm)
        return 0

    lax.fori_loop(1, 16, spread_w, 0)

    drain(gg.at[pl.ds(0, 15)], rs.at[G])
    igv[...] = dot(place, gg[...].reshape(512, 256))
    pltpu.make_async_copy(igv, ig_ref, out_sem.at[1]).start()
    drain(wd.at[pl.ds(0, 15)], rs.at[WD])
    wgv[...] = wd[...].reshape(256, 256).astype(F32) * (1.0 / 128.0)
    pltpu.make_async_copy(wgv, wg_ref, out_sem.at[2]).start()

    drain(mp_tv, key_ss.at[0])
    drain(mp_mv, key_ss.at[1])
    for p in range(2):
        drain(vall[p].at[pl.ds(5, 5)], adj_ss.at[p])
        drain(fq.at[p, pl.ds(0, 7)], ss.at[F1 + p])
        drain(fr.at[p, pl.ds(0, 3)], ss.at[XF + p])
        drain(xr.at[p, pl.ds(0, 3)], ss.at[XB + p])
        drain(mb.at[p, pl.ds(0, 7)], ss.at[A2S + p])
        c = lax.rem(b - 4 * r - m - 2 * p + 64, 32)

        @pl.when(c // 4 != r)
        def _():
            drain(mb.at[p, 0], ss.at[SELF + p])

    drain(r1r.at[pl.ds(0, 15)], ss.at[R1])
    drain(agg.at[pl.ds(0, 15)], ss.at[R2])
    drain(gg.at[pl.ds(0, 15)], ss.at[G])
    drain(wa.at[pl.ds(0, 3)], ss.at[WA])
    drain(wbr.at[pl.ds(0, 7)], ss.at[WB])
    drain(wc.at[pl.ds(0, 3)], ss.at[WC])
    drain(wd.at[pl.ds(0, 15)], ss.at[WD])
    for i, (src, dst) in enumerate(((hidv, hid_ref), (igv, ig_ref), (wgv, wg_ref))):
        pltpu.make_async_copy(src, dst, out_sem.at[i]).wait()


def hand_over(a0, a1, a2, o0, o1, o2, v0, v1, v2, sem):
    trips = ((a0, v0, o0), (a1, v1, o1), (a2, v2, o2))
    for i, (src, mid, _) in enumerate(trips):
        pltpu.make_async_copy(src, mid, sem.at[i]).start()
    for i, (src, mid, dst) in enumerate(trips):
        pltpu.make_async_copy(src, mid, sem.at[i]).wait()
        pltpu.make_async_copy(mid, dst, sem.at[3 + i]).start()
    for i, (_, mid, dst) in enumerate(trips):
        pltpu.make_async_copy(mid, dst, sem.at[3 + i]).wait()


def shards(x_in, weight, out_grad, adj_vals, adj_tiles, adj_mask, send_rows, send_counts):
    hbm = pl.BlockSpec(memory_space=pltpu.HBM)
    V = pltpu.VMEM
    S = pltpu.SMEM
    I32 = jnp.int32
    dma = pltpu.SemaphoreType.DMA
    outs = (
        jax.ShapeDtypeStruct((512, 256), BF),
        jax.ShapeDtypeStruct((256, 256), F32),
        jax.ShapeDtypeStruct((320, 256), F32),
    )
    results = pl.pallas_call(
        kernel,
        out_shape=outs,
        in_specs=[hbm] * 8,
        out_specs=(hbm,) * 3,
        scratch_shapes=[V((11, 128, 128), BF)] * 2
        + [
            V((320, 256), BF),
            V((256, 256), BF),
            V((512, 256), BF),
            V((16, 32), I32),
            V((32, 32), I32),
            S((4, 2, 5), I32),
            S((4, 5), I32),
            V((4, 2, 5), I32),
            V((4, 5), I32),
            S((4, 2, 5), I32),
            S((4, 5), I32),
            V((2, 512, 512), BF),
            V((2, 512, 512), BF),
            V((16, 16, 256), BF),
            V((2, 8, 16, 256), BF),
            V((2, 4, 8, 16, 256), BF),
            V((2, 16, 2, 16, 256), BF),
            V((16, 32, 256), BF),
            V((16, 32, 256), BF),
            V((16, 32, 256), BF),
            V((512, 256), BF),
            V((512, 256), BF),
            V((2, 2, 24, 16, 256), BF),
            V((2, 4, 8, 16, 256), BF),
            V((2, 8, 16, 256), BF),
            V((2, 8, 16, 256), BF),
            V((16, 2, 16, 256), BF),
            V((8, 16, 256), F32),
            V((4, 8, 128), F32),
            V((4, 8, 128), F32),
            V((8, 128), F32),
            V((8, 8, 128), F32),
            V((4, 8, 128), F32),
            V((16, 16, 256), BF),
            V((512, 256), BF),
            V((256, 256), F32),
            V((320, 256), F32),
            dma((2,)),
            dma((7,)),
            dma((3,)),
            dma((2,)),
            dma((2,)),
            dma((2,)),
            dma((2,)),
            dma((2,)),
            dma((18,)),
            dma((18,)),
        ],
        compiler_params=pltpu.CompilerParams(
            collective_id=0, has_side_effects=True, vmem_limit_bytes=62 * 1024 * 1024
        ),
        name="graph_layer",
    )(
        jnp.swapaxes(adj_tiles[0], 1, 2),
        adj_mask[0],
        x_in,
        weight,
        out_grad,
        send_rows[0].T,
        send_counts,
        adj_vals[0],
    )
    return pl.pallas_call(
        hand_over,
        out_shape=outs,
        in_specs=[pl.BlockSpec(memory_space=pl.ANY)] * 3,
        out_specs=(hbm,) * 3,
        scratch_shapes=[V(o.shape, o.dtype) for o in outs] + [dma((6,))],
        compiler_params=pltpu.CompilerParams(vmem_limit_bytes=62 * 1024 * 1024),
        name="hand_over",
    )(*results)


def solution(mesh):
    placed = (
        P("blk", None),
        P(),
        P("blk", None),
        P("blk", "rep", "mp", None, None),
        P("blk", "rep", "mp", None),
        P("blk", "rep", "mp"),
        P("blk", None, None),
        P(),
    )
    return jax.shard_map(
        shards,
        mesh=mesh,
        in_specs=placed,
        out_specs=(P("blk", None), P(), P("blk", None)),
        check_vma=False,
    )
```

```python
import functools

import jax
import jax.numpy as jnp
from jax import lax
from jax.experimental import pallas as pl
from jax.experimental.pallas import tpu as pltpu
from jax.sharding import PartitionSpec as P

MESH = pl.DeviceIdType.MESH
BF = jnp.bfloat16
F32 = jnp.float32


def dot(a, b, dims=((1,), (0,))):
    return lax.dot_general(a, b, (dims, ((), ())), preferred_element_type=F32)


def send(src, dst, ssem, rsem, **where):
    pltpu.make_async_remote_copy(
        src_ref=src,
        dst_ref=dst,
        send_sem=ssem,
        recv_sem=rsem,
        device_id=where,
        device_id_type=MESH,
    ).start()


def drain(ref, sem):
    pltpu.make_async_copy(ref, ref, sem).wait()


def kernel(
    tiles_ref,
    mask_ref,
    x_ref,
    w_ref,
    og_ref,
    rows_ref,
    counts_ref,
    adj_ref,
    hid_ref,
    rowr_ref,
    gg_ref,
    wd_ref,
    v0, v1,
    xv, wv, ogv, rowsv, countsv,
    own_ts, own_ms, mp_tv, mp_mv, mp_ts, mp_ms,
    dense, denset,
    outg, fq, fr, nat,
    r1s, r1r, agg,
    pg, gb,
    pb, xr, mb, ar, gv,
    wprod, wa, war, wb, wbr, wc, wdv,
    hidv, rowrv,
    loc_sem, in_sem, out_sem, adj_ss, adj_rs, key_ss, key_rs, key_ls,
    ss, rs,
):
    vall = (v0, v1)
    b = lax.axis_index("blk")
    r = lax.axis_index("rep")
    m = lax.axis_index("mp")
    z = b // 2
    parity = lax.rem(b, 2)
    h = lax.rem(m + b, 2)
    k = r * 2 + m
    kw = r * 2 + h
    quad = lax.rem(b, 4)
    R1, R2, G, WA, WB, WC, WD, A2 = range(8)
    XF, XB, A2S, SELF, F1 = 8, 10, 12, 14, 16

    def at_blk(t):
        return {"blk": t, "mp": lax.rem(h + t, 2)}

    def in_group(d):
        t = lax.rem(k + d, 16)
        return t // 2, lax.rem(t, 2)

    staged = (
        (rows_ref, rowsv),
        (counts_ref, countsv),
        (x_ref, xv),
        (tiles_ref, own_ts),
        (mask_ref, own_ms),
        (w_ref, wv),
        (og_ref, ogv),
    )

    def start(first, end):
        for i in range(first, end):
            src, dst = staged[i]
            pltpu.make_async_copy(src, dst, in_sem.at[i]).start()

    start(0, 3)

    barrier = pltpu.get_barrier_semaphore()

    def greet(where):
        pl.semaphore_signal(barrier, inc=1, device_id=where, device_id_type=MESH)

    def greet_z(n, _):
        greet({"blk": lax.rem(b + 14 - 2 * n, 32)})
        greet({"blk": lax.rem(b + 18 + 2 * n, 32)})
        return 0

    lax.fori_loop(0, 7, greet_z, 0)

    for d in (29, 3, 31, 1):
        greet(at_blk(lax.rem(b + d, 32)))
    greet({"mp": 1 - m})

    def greet_rep(d, _):
        greet({"rep": lax.rem(r + d, 8)})
        return 0

    lax.fori_loop(1, 8, greet_rep, 0)

    start(3, 7)

    def arrived(i):
        src, dst = staged[i]
        pltpu.make_async_copy(src, dst, in_sem.at[i]).wait()

    for p in range(2):
        pltpu.make_async_copy(
            adj_ref.at[m + 2 * p], vall[p].at[pl.ds(0, 5)], loc_sem.at[p]
        ).start()
        vall[p][10] = jnp.zeros((128, 128), BF)

    iota = functools.partial(lax.broadcasted_iota, jnp.int32)
    expand = (2 * (iota((256, 32), 0) // 16) + h == iota((256, 32), 1)).astype(BF)
    in_slot = lax.rem(iota((256, 16), 0), 16) == iota((256, 16), 1)
    mine = (iota((32, 16), 0) == b).astype(BF)
    arrived(0)
    arrived(1)
    counts = countsv[...].astype(F32).astype(BF)
    sent = dot(mine, counts, ((0,), (0,)))
    row = jnp.where(iota((16, 32), 0).astype(F32) < sent, rowsv[...], 384)
    high = (row // 128).astype(F32).astype(BF)
    low = lax.rem(row, 128).astype(F32).astype(BF)
    full = dot(expand, high, ((1,), (1,))) * 128.0 + dot(expand, low, ((1,), (1,)))
    rowc = jnp.sum(jnp.where(in_slot, full, 0.0), axis=1, keepdims=True)
    pick = (rowc == iota((256, 320), 1).astype(F32)).astype(BF)
    arrived(2)
    outg[...] = dot(pick, xv[...]).astype(BF).reshape(16, 16, 256)

    pl.semaphore_wait(barrier, 26)

    def owner_at(d):
        return lax.rem(2 * lax.rem(z + d, 16) + parity - 4 * r - m + 64, 32) // 2

    def deliver(far):
        def one(n, _):
            up = 7 - n
            low, top = F1 + 1 - far, F1 + 2 + far
            send(
                outg.at[owner_at(up)],
                fq.at[0, n],
                ss.at[low],
                rs.at[low],
                blk=lax.rem(b + 2 * up, 32),
            )
            send(
                outg.at[owner_at(8 + n)],
                fq.at[1, 7 - n],
                ss.at[top],
                rs.at[top],
                blk=lax.rem(b + 2 * (9 + n), 32),
            )
            return 0

        lax.fori_loop(*((0, 4) if far else (4, 7)), one, 0)

    deliver(1)
    deliver(0)

    send(tiles_ref, mp_tv, key_ss.at[0], key_rs.at[0], mp=1 - m)
    send(mask_ref, mp_mv, key_ss.at[1], key_rs.at[1], mp=1 - m)
    for p in range(2):
        send(
            adj_ref.at[1 - m + 2 * p],
            vall[p].at[pl.ds(5, 5)],
            adj_ss.at[p],
            adj_rs.at[p],
            mp=1 - m,
        )
    fq[0, 7] = outg[owner_at(0)]
    fq[1, 0] = outg[owner_at(15)]

    def first_z(t, j):
        return lax.rem(t // 2 + (9 if j < 2 else 0), 16)

    held = dot(counts, mine)
    expand_r = (iota((512, 32), 0) // 16 == iota((512, 32), 1)).astype(BF)
    in_slot_r = lax.rem(iota((512, 16), 0), 16) == iota((512, 16), 1)
    alive = dot(expand_r, (iota((32, 16), 1).astype(F32) < held).astype(BF))
    live = jnp.sum(jnp.where(in_slot_r, alive, 0.0), axis=1, keepdims=True) > 0.5
    at = iota((32, 512), 1)
    owner = 4 * (at // 64) + 2 * lax.rem(at // 16, 2) + lax.rem(at // 32, 2)
    expand_t = (owner == iota((32, 512), 0)).astype(BF)
    in_slot_t = lax.rem(iota((16, 512), 1), 16) == iota((16, 512), 0)
    full_t = dot(high, expand_t) * 128.0 + dot(low, expand_t)
    rowrv[...] = jnp.sum(jnp.where(in_slot_t, full_t, 0.0), axis=0, keepdims=True)
    pltpu.make_async_copy(rowrv, rowr_ref, out_sem.at[1]).start()

    arrived(3)
    arrived(4)
    drain(mp_tv, key_rs.at[0])
    drain(mp_mv, key_rs.at[1])
    for i, (src, dst) in enumerate(((mp_tv, mp_ts), (mp_mv, mp_ms))):
        pltpu.make_async_copy(src, dst, key_ls.at[i]).start()
    for i, (src, dst) in enumerate(((mp_tv, mp_ts), (mp_mv, mp_ms))):
        pltpu.make_async_copy(src, dst, key_ls.at[i]).wait()

    def build(p):
        j = m + 2 * p
        pltpu.make_async_copy(
            adj_ref.at[m + 2 * p], vall[p].at[pl.ds(0, 5)], loc_sem.at[p]
        ).wait()
        drain(vall[p].at[pl.ds(5, 5)], adj_rs.at[p])

        def places(ts, ms):
            return [
                jnp.where(ms[j, t] == 1, ts[j, 0, t] * 4 + ts[j, 1, t], 16) for t in range(5)
            ]

        own, other = places(own_ts, own_ms), places(mp_ts, mp_ms)
        for row in range(4):
            for col in range(4):
                at = jnp.int32(10)
                for t in range(5):
                    at = jnp.where(own[t] == row * 4 + col, t, at)
                    at = jnp.where(other[t] == row * 4 + col, 5 + t, at)
                tile = vall[p][at]
                dense[p, row * 128:(row + 1) * 128, col * 128:(col + 1) * 128] = tile

    def transpose(p):
        for row in range(4):
            for col in range(4):
                tile = dense[p, row * 128:(row + 1) * 128, col * 128:(col + 1) * 128]
                denset[p, col * 128:(col + 1) * 128, row * 128:(row + 1) * 128] = tile.T

    def others(p):
        for q, to in ((p, 1 - m + 2 * p), (1 - p, 2 * p), (1 - p, 2 * p + 1)):
            yield q, to, lax.rem(b - m - 2 * q + to + 32, 32)

    for far in (1, 0):
        for p in range(2):
            sem = F1 + 2 * p + (far if p else 1 - far)
            drain(fq.at[p, pl.ds(0, 3 + far)], rs.at[sem])
        for p in range(2):
            for q, to, t in others(p):
                piece = pl.ds(4 * (far if q else 1 - far), 4)
                send(
                    fq.at[q, piece],
                    fr.at[p, m + 2 * q, piece],
                    ss.at[XF + q],
                    rs.at[XF + p],
                    **at_blk(t),
                )
    for p in range(2):
        fr[p, m + 2 * p] = fq[p]

    build(0)
    build(1)
    part = None
    for p in range(2):
        drain(fr.at[p, pl.ds(0, 3)], rs.at[XF + p])
        for j in range(4):
            t = lax.rem(b - m - 2 * p + j + 32, 32)
            for n in range(8):
                nat[p, lax.rem(first_z(t, j) + n, 16), lax.rem(t, 2)] = fr[p, j, n]
        term = dot(dense[p], nat[p].reshape(512, 256))
        part = term if part is None else part + term

    r1s[...] = part.astype(BF).reshape(16, 32, 256)

    def scatter(d, _):
        tr, tm = in_group(d)
        send(r1s.at[2 * tr + tm], r1r.at[k], ss.at[R1], rs.at[R1], rep=tr, mp=tm)
        return 0

    lax.fori_loop(1, 16, scatter, 0)
    r1r[k] = r1s[k]
    transpose(0)
    drain(r1r.at[pl.ds(0, 15)], rs.at[R1])
    total = r1r[0].astype(F32)
    for i in range(1, 16):
        total += r1r[i].astype(F32)
    agg[k] = total.astype(BF)

    def gather(d, _):
        tr, tm = in_group(d)
        send(agg.at[k], agg.at[k], ss.at[R2], rs.at[R2], rep=tr, mp=tm)
        return 0

    lax.fori_loop(1, 16, gather, 0)
    transpose(1)
    arrived(5)
    arrived(6)
    drain(agg.at[pl.ds(0, 15)], rs.at[R2])

    for q in range(4):
        rows = slice(q * 128, (q + 1) * 128)
        preact = dot(agg[4 * q:4 * q + 4].reshape(128, 256), wv[...])
        gate = jax.nn.sigmoid(preact)
        hidv[rows, :] = jnp.where(live[rows], preact * gate, 0.0).astype(BF)
        slope = gate * (1.0 + preact * (1.0 - gate))
        pre = jnp.where(live[rows], ogv[rows, :].astype(F32) * slope, 0.0).astype(BF)
        pg[rows, :] = pre
        gb[rows, :] = dot(pre, wv[...], ((1,), (1,))).astype(BF)

    columns = pl.ds(pl.multiple_of((r // 4) * 128, 128), 128)
    wprod[...] = dot(agg[:, :, columns].reshape(512, 128), pg[...], ((0,), (0,))).reshape(8, 16, 256)
    w16 = wprod[lax.rem(r, 4) * 2 + h]
    for a in range(2):
        for c in range(2):
            wa[2 * a + c] = w16[a * 8:(a + 1) * 8, c * 128:(c + 1) * 128]
    war[quad] = wa[quad]
    for e in range(1, 4):
        q = lax.rem(quad + e, 4)
        send(wa.at[q], war.at[quad], ss.at[WA], rs.at[WA], **at_blk(b - quad + q))
    eighth = b // 4

    for p in range(2):
        terms = dot(denset[p], gb[...]).astype(BF).reshape(16, 2, 16, 256)
        for q in range(2):
            pb[p, q, 0:16] = terms[:, q]
            pb[p, q, 16:24] = terms[0:8, q]
        xr[p, m + 2 * p] = pb[p, parity, pl.ds(first_z(b, 2 * p), 8)]
    for p in range(2):
        for q, to, t in others(p):
            send(
                pb.at[q, lax.rem(t, 2), pl.ds(first_z(t, 2 * p), 8)],
                xr.at[p, m + 2 * q],
                ss.at[XB + q],
                rs.at[XB + p],
                **at_blk(t),
            )
    pltpu.make_async_copy(hidv, hid_ref, out_sem.at[0]).start()

    drain(war.at[pl.ds(0, 3)], rs.at[WA])
    tile = war[0] + war[1] + war[2] + war[3]
    wb[...] = tile
    wbr[eighth] = tile
    for e in range(1, 8):
        send(wb, wbr.at[eighth], ss.at[WB], rs.at[WB], blk=lax.rem(b + 4 * e, 32))

    for p in range(2):
        drain(xr.at[p, pl.ds(0, 3)], rs.at[XB + p])
        total = xr[p, 0].astype(F32)
        for i in range(1, 4):
            total += xr[p, i].astype(F32)
        mb[p] = total.astype(BF)
        c = lax.rem(b - 4 * r - m - 2 * p + 64, 32)
        home, slot = c // 4, lax.rem(c, 4) // 2

        def back(n, _):
            away = 7 - n
            send(
                mb.at[p, n if p == 0 else away],
                ar.at[slot, r],
                ss.at[A2S + p],
                rs.at[A2],
                blk=lax.rem(b + (32 - 2 * away if p == 0 else 2 * away), 32),
                rep=home,
            )
            return 0

        lax.fori_loop(0, 7, back, 0)
        here = 7 if p == 0 else 0

        @pl.when(home == r)
        def _():
            pltpu.make_async_copy(mb.at[p, here], ar.at[slot, r], rs.at[A2]).start()

        @pl.when(home != r)
        def _():
            send(mb.at[p, here], ar.at[slot, r], ss.at[SELF + p], rs.at[A2], rep=home)

    drain(wbr.at[pl.ds(0, 7)], rs.at[WB])
    tile = wbr[0]
    for i in range(1, 8):
        tile += wbr[i]
    wc[quad] = tile
    for e in range(1, 4):
        q = lax.rem(quad + e, 4)
        send(wc.at[quad], wc.at[quad], ss.at[WC], rs.at[WC], **at_blk(b - quad + q))

    drain(wc.at[pl.ds(0, 3)], rs.at[WC])
    for a in range(2):
        for c in range(2):
            w_part = wc[2 * a + c]
            wprod[0, a * 8:(a + 1) * 8, c * 128:(c + 1) * 128] = w_part
    wdv[...] = wprod[0].astype(BF)
    pltpu.make_async_copy(wdv, wd_ref.at[kw], rs.at[WD]).start()

    def spread_w(d, _):
        tr, tm = in_group(d)
        send(wdv, wd_ref.at[kw], ss.at[WD], rs.at[WD], rep=tr, mp=tm)
        return 0

    lax.fori_loop(1, 16, spread_w, 0)

    drain(ar, rs.at[A2])
    total = ar[:, 0].astype(F32)
    for i in range(1, 8):
        total += ar[:, i].astype(F32)
    gv[...] = total.astype(BF)
    pltpu.make_async_copy(gv, gg_ref.at[kw], rs.at[G]).start()

    def share(d, _):
        tr, tm = in_group(d)
        send(gv, gg_ref.at[kw], ss.at[G], rs.at[G], rep=tr, mp=tm)
        return 0

    lax.fori_loop(1, 16, share, 0)

    drain(wd_ref, rs.at[WD])
    drain(gg_ref, rs.at[G])

    drain(mp_tv, key_ss.at[0])
    drain(mp_mv, key_ss.at[1])
    for p in range(2):
        drain(vall[p].at[pl.ds(5, 5)], adj_ss.at[p])
        drain(fq.at[p, pl.ds(0, 4 if p == 0 else 3)], ss.at[F1 + 2 * p])
        drain(fq.at[p, pl.ds(0, 3 if p == 0 else 4)], ss.at[F1 + 2 * p + 1])
        drain(fr.at[p, pl.ds(0, 3)], ss.at[XF + p])
        drain(xr.at[p, pl.ds(0, 3)], ss.at[XB + p])
        drain(mb.at[p, pl.ds(0, 7)], ss.at[A2S + p])
        c = lax.rem(b - 4 * r - m - 2 * p + 64, 32)

        @pl.when(c // 4 != r)
        def _():
            drain(mb.at[p, 0], ss.at[SELF + p])

    drain(r1r.at[pl.ds(0, 15)], ss.at[R1])
    drain(agg.at[pl.ds(0, 15)], ss.at[R2])
    drain(gg_ref.at[pl.ds(0, 15)], ss.at[G])
    drain(wa.at[pl.ds(0, 3)], ss.at[WA])
    drain(wbr.at[pl.ds(0, 7)], ss.at[WB])
    drain(wc.at[pl.ds(0, 3)], ss.at[WC])
    drain(wd_ref.at[pl.ds(0, 15)], ss.at[WD])
    for i, (src, dst) in enumerate(((hidv, hid_ref), (rowrv, rowr_ref))):
        pltpu.make_async_copy(src, dst, out_sem.at[i]).wait()


def finish(hid_in, rowr_in, gg_in, wd_in, hid_ref, wg_ref, ig_ref, hid, rowr, gg, wd, wg, ig, sem):
    incoming = ((rowr_in, rowr), (gg_in, gg), (wd_in, wd), (hid_in, hid))
    outgoing = ((ig, ig_ref), (wg, wg_ref), (hid, hid_ref))
    for i, (src, dst) in enumerate(incoming):
        pltpu.make_async_copy(src, dst, sem.at[i]).start()

    def arrived(i):
        src, dst = incoming[i]
        pltpu.make_async_copy(src, dst, sem.at[i]).wait()

    arrived(0)
    place = (rowr[...] == lax.broadcasted_iota(jnp.int32, (320, 512), 0).astype(F32)).astype(BF)
    arrived(1)
    ig[...] = dot(place, gg[...].reshape(512, 256))
    pltpu.make_async_copy(*outgoing[0], sem.at[4]).start()
    arrived(2)
    wg[...] = wd[...].reshape(256, 256).astype(F32) * (1.0 / 128.0)
    pltpu.make_async_copy(*outgoing[1], sem.at[5]).start()
    arrived(3)
    pltpu.make_async_copy(*outgoing[2], sem.at[6]).start()
    for i, (src, dst) in enumerate(outgoing):
        pltpu.make_async_copy(src, dst, sem.at[4 + i]).wait()


def shards(x_in, weight, out_grad, adj_vals, adj_tiles, adj_mask, send_rows, send_counts):
    hbm = pl.BlockSpec(memory_space=pltpu.HBM)
    V = pltpu.VMEM
    S = pltpu.SMEM
    I32 = jnp.int32
    dma = pltpu.SemaphoreType.DMA
    outs = (
        jax.ShapeDtypeStruct((512, 256), BF),
        jax.ShapeDtypeStruct((256, 256), F32),
        jax.ShapeDtypeStruct((320, 256), F32),
    )
    between = (
        jax.ShapeDtypeStruct((512, 256), BF),
        jax.ShapeDtypeStruct((1, 512), F32),
        jax.ShapeDtypeStruct((16, 2, 16, 256), BF),
        jax.ShapeDtypeStruct((16, 16, 256), BF),
    )
    results = pl.pallas_call(
        kernel,
        out_shape=between,
        in_specs=[hbm] * 8,
        out_specs=(hbm,) * 4,
        scratch_shapes=[V((11, 128, 128), BF)] * 2
        + [
            V((320, 256), BF),
            V((256, 256), BF),
            V((512, 256), BF),
            V((16, 32), I32),
            V((32, 32), I32),
            S((4, 2, 5), I32),
            S((4, 5), I32),
            V((4, 2, 5), I32),
            V((4, 5), I32),
            S((4, 2, 5), I32),
            S((4, 5), I32),
            V((2, 512, 512), BF),
            V((2, 512, 512), BF),
            V((16, 16, 256), BF),
            V((2, 8, 16, 256), BF),
            V((2, 4, 8, 16, 256), BF),
            V((2, 16, 2, 16, 256), BF),
            V((16, 32, 256), BF),
            V((16, 32, 256), BF),
            V((16, 32, 256), BF),
            V((512, 256), BF),
            V((512, 256), BF),
            V((2, 2, 24, 16, 256), BF),
            V((2, 4, 8, 16, 256), BF),
            V((2, 8, 16, 256), BF),
            V((2, 8, 16, 256), BF),
            V((2, 16, 256), BF),
            V((8, 16, 256), F32),
            V((4, 8, 128), F32),
            V((4, 8, 128), F32),
            V((8, 128), F32),
            V((8, 8, 128), F32),
            V((4, 8, 128), F32),
            V((16, 256), BF),
            V((512, 256), BF),
            V((1, 512), F32),
            dma((2,)),
            dma((7,)),
            dma((2,)),
            dma((2,)),
            dma((2,)),
            dma((2,)),
            dma((2,)),
            dma((2,)),
            dma((20,)),
            dma((20,)),
        ],
        compiler_params=pltpu.CompilerParams(
            collective_id=0, has_side_effects=True, vmem_limit_bytes=62 * 1024 * 1024
        ),
        name="graph_layer",
    )(
        jnp.swapaxes(adj_tiles[0], 1, 2),
        adj_mask[0],
        x_in,
        weight,
        out_grad,
        send_rows[0].T,
        send_counts,
        adj_vals[0],
    )
    return pl.pallas_call(
        finish,
        out_shape=outs,
        in_specs=[hbm] * 4,
        out_specs=(hbm,) * 3,
        scratch_shapes=[V(o.shape, o.dtype) for o in between + outs[1:]] + [dma((7,))],
        compiler_params=pltpu.CompilerParams(vmem_limit_bytes=62 * 1024 * 1024),
        name="finish",
    )(*results)


def solution(mesh):
    placed = (
        P("blk", None),
        P(),
        P("blk", None),
        P("blk", "rep", "mp", None, None),
        P("blk", "rep", "mp", None),
        P("blk", "rep", "mp"),
        P("blk", None, None),
        P(),
    )
    return jax.shard_map(
        shards,
        mesh=mesh,
        in_specs=placed,
        out_specs=(P("blk", None), P(), P("blk", None)),
        check_vma=False,
    )
```

```python
import functools

import jax
import jax.numpy as jnp
from jax import lax
from jax.experimental import pallas as pl
from jax.experimental.pallas import tpu as pltpu
from jax.sharding import PartitionSpec as P

MESH = pl.DeviceIdType.MESH
BF = jnp.bfloat16
F32 = jnp.float32


def dot(a, b, dims=((1,), (0,))):
    return lax.dot_general(a, b, (dims, ((), ())), preferred_element_type=F32)


def send(src, dst, ssem, rsem, **where):
    pltpu.make_async_remote_copy(
        src_ref=src,
        dst_ref=dst,
        send_sem=ssem,
        recv_sem=rsem,
        device_id=where,
        device_id_type=MESH,
    ).start()


def drain(ref, sem):
    pltpu.make_async_copy(ref, ref, sem).wait()


def kernel(
    tiles_ref,
    mask_ref,
    x_ref,
    w_ref,
    og_ref,
    rows_ref,
    counts_ref,
    adj_ref,
    hid_ref,
    rowr_ref,
    gg_ref,
    wd_ref,
    v0, v1,
    xv, wv, ogv, rowsv, countsv,
    own_ts, own_ms, mp_tv, mp_mv, mp_ts, mp_ms,
    dense, denset,
    outg, fq, fr, nat,
    r1s, r1r, agg,
    pg, gb,
    pb, xr, mb, ar, gv,
    wprod, wa, war, wb, wbr, wc, wdv,
    hidv, rowrv,
    loc_sem, in_sem, out_sem, adj_ss, adj_rs, key_ss, key_rs, key_ls,
    ss, rs,
):
    vall = (v0, v1)
    b = lax.axis_index("blk")
    r = lax.axis_index("rep")
    m = lax.axis_index("mp")
    z = b // 2
    parity = lax.rem(b, 2)
    h = lax.rem(m + b, 2)
    k = r * 2 + m
    kw = r * 2 + h
    quad = lax.rem(b, 4)
    R1, R2, G, WA, WB, WC, WD, A2 = range(8)
    XF, XS, A2S, SELF, F1, XB = 8, 10, 12, 14, 16, 20

    def at_blk(t):
        return {"blk": t, "mp": lax.rem(h + t, 2)}

    def in_group(n):
        d = 8 + jnp.where(lax.rem(n, 2) == 0, -(n // 2), n // 2 + 1)
        t = lax.rem(k + d, 16)
        return t // 2, lax.rem(t, 2)

    staged = (
        (rows_ref, rowsv),
        (counts_ref, countsv),
        (x_ref, xv),
        (tiles_ref, own_ts),
        (mask_ref, own_ms),
        (w_ref, wv),
        (og_ref, ogv),
    )

    def start(first, end):
        for i in range(first, end):
            src, dst = staged[i]
            pltpu.make_async_copy(src, dst, in_sem.at[i]).start()

    def arrived(i):
        src, dst = staged[i]
        pltpu.make_async_copy(src, dst, in_sem.at[i]).wait()

    start(0, 3)

    barrier = pltpu.get_barrier_semaphore()

    def greet(where):
        pl.semaphore_signal(barrier, inc=1, device_id=where, device_id_type=MESH)

    def greet_z(n, _):
        greet({"blk": lax.rem(b + 14 - 2 * n, 32)})
        greet({"blk": lax.rem(b + 18 + 2 * n, 32)})
        return 0

    lax.fori_loop(0, 7, greet_z, 0)

    for d in (29, 3, 31, 1):
        greet(at_blk(lax.rem(b + d, 32)))
    greet({"mp": 1 - m})

    def greet_rep(d, _):
        greet({"rep": lax.rem(r + d, 8)})
        return 0

    lax.fori_loop(1, 8, greet_rep, 0)

    iota = functools.partial(lax.broadcasted_iota, jnp.int32)
    expand = (2 * (iota((256, 32), 0) // 16) + h == iota((256, 32), 1)).astype(BF)
    in_slot = lax.rem(iota((256, 16), 0), 16) == iota((256, 16), 1)
    mine = (iota((32, 16), 0) == b).astype(BF)
    arrived(0)
    arrived(1)
    counts = countsv[...].astype(F32).astype(BF)
    sent = dot(mine, counts, ((0,), (0,)))
    row = jnp.where(iota((16, 32), 0).astype(F32) < sent, rowsv[...], 384)
    high = (row // 128).astype(F32).astype(BF)
    low = lax.rem(row, 128).astype(F32).astype(BF)
    full = dot(expand, high, ((1,), (1,))) * 128.0 + dot(expand, low, ((1,), (1,)))
    rowc = jnp.sum(jnp.where(in_slot, full, 0.0), axis=1, keepdims=True)
    pick = (rowc == iota((256, 320), 1).astype(F32)).astype(BF)
    arrived(2)
    outg[...] = dot(pick, xv[...]).astype(BF).reshape(16, 16, 256)

    pl.semaphore_wait(barrier, 26)

    def owner_at(d):
        return lax.rem(2 * lax.rem(z + d, 16) + parity - 4 * r - m + 64, 32) // 2

    def half(p, far):
        i = far if p else 1 - far
        return i, pl.ds(4 * i, 4)

    def deliver(far):
        low, top = F1 + half(0, far)[0], F1 + 2 + half(1, far)[0]

        def one(n, _):
            up = 7 - n
            send(
                outg.at[owner_at(up)],
                fq.at[0, n],
                ss.at[low],
                rs.at[low],
                blk=lax.rem(b + 2 * up, 32),
            )
            send(
                outg.at[owner_at(8 + n)],
                fq.at[1, 7 - n],
                ss.at[top],
                rs.at[top],
                blk=lax.rem(b + 2 * (9 + n), 32),
            )
            return 0

        lax.fori_loop(*((0, 4) if far else (4, 7)), one, 0)

    deliver(0)
    deliver(1)

    send(tiles_ref, mp_tv, key_ss.at[0], key_rs.at[0], mp=1 - m)
    send(mask_ref, mp_mv, key_ss.at[1], key_rs.at[1], mp=1 - m)
    for p in range(2):
        send(
            adj_ref.at[1 - m + 2 * p],
            vall[p].at[pl.ds(5, 5)],
            adj_ss.at[p],
            adj_rs.at[p],
            mp=1 - m,
        )
    fq[0, 7] = outg[owner_at(0)]
    fq[1, 0] = outg[owner_at(15)]

    def first_z(t, j):
        return lax.rem(t // 2 + (9 if j < 2 else 0), 16)

    start(3, 7)

    for p in range(2):
        pltpu.make_async_copy(
            adj_ref.at[m + 2 * p], vall[p].at[pl.ds(0, 5)], loc_sem.at[p]
        ).start()
        vall[p][10] = jnp.zeros((128, 128), BF)

    held = dot(counts, mine)
    expand_r = (iota((512, 32), 0) // 16 == iota((512, 32), 1)).astype(BF)
    in_slot_r = lax.rem(iota((512, 16), 0), 16) == iota((512, 16), 1)
    alive = dot(expand_r, (iota((32, 16), 1).astype(F32) < held).astype(BF))
    live = jnp.sum(jnp.where(in_slot_r, alive, 0.0), axis=1, keepdims=True) > 0.5
    at = iota((32, 512), 1)
    owner = 4 * (at // 64) + 2 * lax.rem(at // 16, 2) + lax.rem(at // 32, 2)
    expand_t = (owner == iota((32, 512), 0)).astype(BF)
    in_slot_t = lax.rem(iota((16, 512), 1), 16) == iota((16, 512), 0)
    full_t = dot(high, expand_t) * 128.0 + dot(low, expand_t)
    rowrv[...] = jnp.sum(jnp.where(in_slot_t, full_t, 0.0), axis=0, keepdims=True)
    pltpu.make_async_copy(rowrv, rowr_ref, out_sem.at[1]).start()

    arrived(3)
    arrived(4)
    drain(mp_tv, key_rs.at[0])
    drain(mp_mv, key_rs.at[1])
    for i, (src, dst) in enumerate(((mp_tv, mp_ts), (mp_mv, mp_ms))):
        pltpu.make_async_copy(src, dst, key_ls.at[i]).start()
    for i, (src, dst) in enumerate(((mp_tv, mp_ts), (mp_mv, mp_ms))):
        pltpu.make_async_copy(src, dst, key_ls.at[i]).wait()

    def build(p):
        j = m + 2 * p
        pltpu.make_async_copy(
            adj_ref.at[m + 2 * p], vall[p].at[pl.ds(0, 5)], loc_sem.at[p]
        ).wait()
        drain(vall[p].at[pl.ds(5, 5)], adj_rs.at[p])

        def places(ts, ms):
            return [
                jnp.where(ms[j, t] == 1, ts[j, 0, t] * 4 + ts[j, 1, t], 16) for t in range(5)
            ]

        own, other = places(own_ts, own_ms), places(mp_ts, mp_ms)
        for row in range(4):
            for col in range(4):
                at = jnp.int32(10)
                for t in range(5):
                    at = jnp.where(own[t] == row * 4 + col, t, at)
                    at = jnp.where(other[t] == row * 4 + col, 5 + t, at)
                tile = vall[p][at]
                dense[p, row * 128:(row + 1) * 128, col * 128:(col + 1) * 128] = tile

    def transpose(p):
        for row in range(4):
            for col in range(4):
                tile = dense[p, row * 128:(row + 1) * 128, col * 128:(col + 1) * 128]
                denset[p, col * 128:(col + 1) * 128, row * 128:(row + 1) * 128] = tile.T

    def others(p):
        for q, to in ((p, 1 - m + 2 * p), (1 - p, 1 - m + 2 * p), (1 - p, m + 2 * p)):
            yield q, to, lax.rem(b - m - 2 * q + to + 32, 32)

    for far in (0, 1):
        for p in range(2):
            drain(fq.at[p, pl.ds(0, 3 + far)], rs.at[F1 + 2 * p + half(p, far)[0]])
        for p in range(2):
            for q, to, t in others(p):
                piece = half(q, far)[1]
                send(
                    fq.at[q, piece],
                    fr.at[p, m + 2 * q, piece],
                    ss.at[XF + q],
                    rs.at[XF + p],
                    **at_blk(t),
                )
    for p in range(2):
        fr[p, m + 2 * p] = fq[p]

    build(0)
    build(1)
    part = None
    for p in range(2):
        drain(fr.at[p, pl.ds(0, 3)], rs.at[XF + p])
        for j in range(4):
            t = lax.rem(b - m - 2 * p + j + 32, 32)
            for n in range(8):
                nat[p, lax.rem(first_z(t, j) + n, 16), lax.rem(t, 2)] = fr[p, j, n]
        term = dot(dense[p], nat[p].reshape(512, 256))
        part = term if part is None else part + term

    r1s[...] = part.astype(BF).reshape(16, 32, 256)

    def scatter(d, _):
        tr, tm = in_group(d)
        send(r1s.at[2 * tr + tm], r1r.at[k], ss.at[R1], rs.at[R1], rep=tr, mp=tm)
        return 0

    lax.fori_loop(0, 15, scatter, 0)
    r1r[k] = r1s[k]
    transpose(0)
    drain(r1r.at[pl.ds(0, 15)], rs.at[R1])
    total = r1r[0].astype(F32)
    for i in range(1, 16):
        total += r1r[i].astype(F32)
    agg[k] = total.astype(BF)

    def gather(d, _):
        tr, tm = in_group(d)
        send(agg.at[k], agg.at[k], ss.at[R2], rs.at[R2], rep=tr, mp=tm)
        return 0

    lax.fori_loop(0, 15, gather, 0)
    transpose(1)
    arrived(5)
    arrived(6)
    drain(agg.at[pl.ds(0, 15)], rs.at[R2])

    for q in range(4):
        rows = slice(q * 128, (q + 1) * 128)
        preact = dot(agg[4 * q:4 * q + 4].reshape(128, 256), wv[...])
        gate = jax.nn.sigmoid(preact)
        hidv[rows, :] = jnp.where(live[rows], preact * gate, 0.0).astype(BF)
        slope = gate * (1.0 + preact * (1.0 - gate))
        pre = jnp.where(live[rows], ogv[rows, :].astype(F32) * slope, 0.0).astype(BF)
        pg[rows, :] = pre
        gb[rows, :] = dot(pre, wv[...], ((1,), (1,))).astype(BF)

    columns = pl.ds(pl.multiple_of((r // 4) * 128, 128), 128)
    wprod[...] = dot(agg[:, :, columns].reshape(512, 128), pg[...], ((0,), (0,))).reshape(8, 16, 256)
    w16 = wprod[lax.rem(r, 4) * 2 + h]
    for a in range(2):
        for c in range(2):
            wa[2 * a + c] = w16[a * 8:(a + 1) * 8, c * 128:(c + 1) * 128]
    war[quad] = wa[quad]
    for e in range(1, 4):
        q = lax.rem(quad + e, 4)
        send(wa.at[q], war.at[quad], ss.at[WA], rs.at[WA], **at_blk(b - quad + q))
    eighth = b // 4

    for p in range(2):
        terms = dot(denset[p], gb[...]).astype(BF).reshape(16, 2, 16, 256)
        for q in range(2):
            pb[p, q, 0:16] = terms[:, q]
            pb[p, q, 16:24] = terms[0:8, q]
        xr[p, m + 2 * p] = pb[p, parity, pl.ds(first_z(b, 2 * p), 8)]

    def swap_back(far):
        for p in range(2):
            i, piece = half(p, far)
            for q, to, t in others(p):
                send(
                    pb.at[q, lax.rem(t, 2), pl.ds(first_z(t, 2 * p) + 4 * i, 4)],
                    xr.at[p, m + 2 * q, piece],
                    ss.at[XS + far],
                    rs.at[XB + 2 * p + i],
                    **at_blk(t),
                )

    swap_back(1)
    pltpu.make_async_copy(hidv, hid_ref, out_sem.at[0]).start()

    drain(war.at[pl.ds(0, 3)], rs.at[WA])
    tile = war[0] + war[1] + war[2] + war[3]
    wb[...] = tile
    wbr[eighth] = tile
    for e in range(1, 8):
        send(wb, wbr.at[eighth], ss.at[WB], rs.at[WB], blk=lax.rem(b + 4 * e, 32))

    drain(xr.at[0, pl.ds(0, 3)], ss.at[XS + 1])
    swap_back(0)

    for far in (1, 0):
        for p in range(2):
            i, piece = half(p, far)
            drain(xr.at[p, pl.ds(0, 3), piece], rs.at[XB + 2 * p + i])
            total = xr[p, 0, piece].astype(F32)
            for n in range(1, 4):
                total += xr[p, n, piece].astype(F32)
            mb[p, piece] = total.astype(BF)
            c = lax.rem(b - 4 * r - m - 2 * p + 64, 32)
            home, slot = c // 4, lax.rem(c, 4) // 2

            def back(n, _):
                away = 7 - n
                send(
                    mb.at[p, n if p == 0 else away],
                    ar.at[slot, r],
                    ss.at[A2S + p],
                    rs.at[A2],
                    blk=lax.rem(b + (32 - 2 * away if p == 0 else 2 * away), 32),
                    rep=home,
                )
                return 0

            lax.fori_loop(*((0, 4) if far else (4, 7)), back, 0)
            if far:
                continue
            here = 7 if p == 0 else 0

            @pl.when(home == r)
            def _():
                pltpu.make_async_copy(mb.at[p, here], ar.at[slot, r], rs.at[A2]).start()

            @pl.when(home != r)
            def _():
                send(mb.at[p, here], ar.at[slot, r], ss.at[SELF + p], rs.at[A2], rep=home)

    drain(wbr.at[pl.ds(0, 7)], rs.at[WB])
    tile = wbr[0]
    for i in range(1, 8):
        tile += wbr[i]
    wc[quad] = tile
    for e in range(1, 4):
        q = lax.rem(quad + e, 4)
        send(wc.at[quad], wc.at[quad], ss.at[WC], rs.at[WC], **at_blk(b - quad + q))

    drain(wc.at[pl.ds(0, 3)], rs.at[WC])
    for a in range(2):
        for c in range(2):
            w_part = wc[2 * a + c]
            wprod[0, a * 8:(a + 1) * 8, c * 128:(c + 1) * 128] = w_part
    wdv[...] = wprod[0].astype(BF)
    pltpu.make_async_copy(wdv, wd_ref.at[kw], rs.at[WD]).start()

    def spread_w(d, _):
        tr, tm = in_group(d)
        send(wdv, wd_ref.at[kw], ss.at[WD], rs.at[WD], rep=tr, mp=tm)
        return 0

    lax.fori_loop(0, 15, spread_w, 0)

    drain(mp_tv, key_ss.at[0])
    drain(mp_mv, key_ss.at[1])
    for p in range(2):
        drain(vall[p].at[pl.ds(5, 5)], adj_ss.at[p])
        for far in (0, 1):
            drain(fq.at[p, pl.ds(0, 3 + far)], ss.at[F1 + 2 * p + half(p, far)[0]])
        drain(fr.at[p, pl.ds(0, 3)], ss.at[XF + p])
    drain(xr.at[0, pl.ds(0, 3)], ss.at[XS])
    drain(r1r.at[pl.ds(0, 15)], ss.at[R1])
    drain(agg.at[pl.ds(0, 15)], ss.at[R2])
    drain(wa.at[pl.ds(0, 3)], ss.at[WA])
    drain(wbr.at[pl.ds(0, 7)], ss.at[WB])
    for i, (src, dst) in enumerate(((hidv, hid_ref), (rowrv, rowr_ref))):
        pltpu.make_async_copy(src, dst, out_sem.at[i]).wait()

    drain(ar, rs.at[A2])
    total = ar[:, 0].astype(F32)
    for i in range(1, 8):
        total += ar[:, i].astype(F32)
    gv[...] = total.astype(BF)
    pltpu.make_async_copy(gv, gg_ref.at[kw], rs.at[G]).start()

    def share(d, _):
        tr, tm = in_group(d)
        send(gv, gg_ref.at[kw], ss.at[G], rs.at[G], rep=tr, mp=tm)
        return 0

    lax.fori_loop(0, 15, share, 0)

    drain(wd_ref, rs.at[WD])
    drain(gg_ref, rs.at[G])

    for p in range(2):
        drain(mb.at[p, pl.ds(0, 7)], ss.at[A2S + p])
        c = lax.rem(b - 4 * r - m - 2 * p + 64, 32)

        @pl.when(c // 4 != r)
        def _():
            drain(mb.at[p, 0], ss.at[SELF + p])

    drain(wc.at[pl.ds(0, 3)], ss.at[WC])
    drain(wd_ref.at[pl.ds(0, 15)], ss.at[WD])
    drain(gg_ref.at[pl.ds(0, 15)], ss.at[G])


def finish(hid_in, rowr_in, gg_in, wd_in, hid_ref, wg_ref, ig_ref, hid, rowr, gg, wd, wg, ig, sem):
    incoming = ((rowr_in, rowr), (gg_in, gg), (wd_in, wd), (hid_in, hid))
    outgoing = ((ig, ig_ref), (wg, wg_ref), (hid, hid_ref))
    for i, (src, dst) in enumerate(incoming):
        pltpu.make_async_copy(src, dst, sem.at[i]).start()

    def arrived(i):
        src, dst = incoming[i]
        pltpu.make_async_copy(src, dst, sem.at[i]).wait()

    arrived(0)
    place = (rowr[...] == lax.broadcasted_iota(jnp.int32, (320, 512), 0).astype(F32)).astype(BF)
    arrived(1)
    ig[...] = dot(place, gg[...].reshape(512, 256))
    pltpu.make_async_copy(*outgoing[0], sem.at[4]).start()
    arrived(2)
    wg[...] = wd[...].reshape(256, 256).astype(F32) * (1.0 / 128.0)
    pltpu.make_async_copy(*outgoing[1], sem.at[5]).start()
    arrived(3)
    pltpu.make_async_copy(*outgoing[2], sem.at[6]).start()
    for i, (src, dst) in enumerate(outgoing):
        pltpu.make_async_copy(src, dst, sem.at[4 + i]).wait()


def shards(x_in, weight, out_grad, adj_vals, adj_tiles, adj_mask, send_rows, send_counts):
    hbm = pl.BlockSpec(memory_space=pltpu.HBM)
    V = pltpu.VMEM
    S = pltpu.SMEM
    I32 = jnp.int32
    dma = pltpu.SemaphoreType.DMA
    outs = (
        jax.ShapeDtypeStruct((512, 256), BF),
        jax.ShapeDtypeStruct((256, 256), F32),
        jax.ShapeDtypeStruct((320, 256), F32),
    )
    between = (
        jax.ShapeDtypeStruct((512, 256), BF),
        jax.ShapeDtypeStruct((1, 512), F32),
        jax.ShapeDtypeStruct((16, 2, 16, 256), BF),
        jax.ShapeDtypeStruct((16, 16, 256), BF),
    )
    results = pl.pallas_call(
        kernel,
        out_shape=between,
        in_specs=[hbm] * 8,
        out_specs=(hbm,) * 4,
        scratch_shapes=[V((11, 128, 128), BF)] * 2
        + [
            V((320, 256), BF),
            V((256, 256), BF),
            V((512, 256), BF),
            V((16, 32), I32),
            V((32, 32), I32),
            S((4, 2, 5), I32),
            S((4, 5), I32),
            V((4, 2, 5), I32),
            V((4, 5), I32),
            S((4, 2, 5), I32),
            S((4, 5), I32),
            V((2, 512, 512), BF),
            V((2, 512, 512), BF),
            V((16, 16, 256), BF),
            V((2, 8, 16, 256), BF),
            V((2, 4, 8, 16, 256), BF),
            V((2, 16, 2, 16, 256), BF),
            V((16, 32, 256), BF),
            V((16, 32, 256), BF),
            V((16, 32, 256), BF),
            V((512, 256), BF),
            V((512, 256), BF),
            V((2, 2, 24, 16, 256), BF),
            V((2, 4, 8, 16, 256), BF),
            V((2, 8, 16, 256), BF),
            V((2, 8, 16, 256), BF),
            V((2, 16, 256), BF),
            V((8, 16, 256), F32),
            V((4, 8, 128), F32),
            V((4, 8, 128), F32),
            V((8, 128), F32),
            V((8, 8, 128), F32),
            V((4, 8, 128), F32),
            V((16, 256), BF),
            V((512, 256), BF),
            V((1, 512), F32),
            dma((2,)),
            dma((7,)),
            dma((2,)),
            dma((2,)),
            dma((2,)),
            dma((2,)),
            dma((2,)),
            dma((2,)),
            dma((24,)),
            dma((24,)),
        ],
        compiler_params=pltpu.CompilerParams(
            collective_id=0, has_side_effects=True, vmem_limit_bytes=62 * 1024 * 1024
        ),
        name="graph_layer",
    )(
        jnp.swapaxes(adj_tiles[0], 1, 2),
        adj_mask[0],
        x_in,
        weight,
        out_grad,
        send_rows[0].T,
        send_counts,
        adj_vals[0],
    )
    return pl.pallas_call(
        finish,
        out_shape=outs,
        in_specs=[hbm] * 4,
        out_specs=(hbm,) * 3,
        scratch_shapes=[V(o.shape, o.dtype) for o in between + outs[1:]] + [dma((7,))],
        compiler_params=pltpu.CompilerParams(vmem_limit_bytes=62 * 1024 * 1024),
        name="finish",
    )(*results)


def solution(mesh):
    placed = (
        P("blk", None),
        P(),
        P("blk", None),
        P("blk", "rep", "mp", None, None),
        P("blk", "rep", "mp", None),
        P("blk", "rep", "mp"),
        P("blk", None, None),
        P(),
    )
    return jax.shard_map(
        shards,
        mesh=mesh,
        in_specs=placed,
        out_specs=(P("blk", None), P(), P("blk", None)),
        check_vma=False,
    )
```

```python
import functools

import jax
import jax.numpy as jnp
from jax import lax
from jax.experimental import pallas as pl
from jax.experimental.pallas import tpu as pltpu
from jax.sharding import PartitionSpec as P

MESH = pl.DeviceIdType.MESH
BF = jnp.bfloat16
F32 = jnp.float32


def dot(a, b, dims=((1,), (0,))):
    return lax.dot_general(a, b, (dims, ((), ())), preferred_element_type=F32)


def send(src, dst, ssem, rsem, **where):
    pltpu.make_async_remote_copy(
        src_ref=src,
        dst_ref=dst,
        send_sem=ssem,
        recv_sem=rsem,
        device_id=where,
        device_id_type=MESH,
    ).start()


def drain(ref, sem):
    pltpu.make_async_copy(ref, ref, sem).wait()


def kernel(
    tiles_ref,
    mask_ref,
    x_ref,
    w_ref,
    og_ref,
    rows_ref,
    counts_ref,
    adj_ref,
    hid_ref,
    rowr_ref,
    gg_ref,
    wd_ref,
    v0, v1,
    xv, wv, ogv, rowsv, countsv,
    own_ts, own_ms, mp_tv, mp_mv, mp_ts, mp_ms,
    dense, denset,
    outg, fq, fr, nat,
    r1s, r1r, agg,
    pg, gb,
    pb, xr, mb, ar, gv,
    wprod, wa, war, wb, wbr, wc, wdv,
    hidv, rowrv,
    loc_sem, in_sem, out_sem, adj_ss, adj_rs, key_ss, key_rs, key_ls,
    ss, rs,
):
    vall = (v0, v1)
    b = lax.axis_index("blk")
    r = lax.axis_index("rep")
    m = lax.axis_index("mp")
    z = b // 2
    parity = lax.rem(b, 2)
    h = lax.rem(m + b, 2)
    k = r * 2 + m
    kw = r * 2 + h
    quad = lax.rem(b, 4)
    R1, R2, G, WA, WB, WC, WD, A2 = range(8)
    XF, XS, A2S, SELF, F1, XB = 8, 10, 12, 14, 16, 20

    def at_blk(t):
        return {"blk": t, "mp": lax.rem(h + t, 2)}

    def in_group(n):
        d = 8 + jnp.where(lax.rem(n, 2) == 0, -(n // 2), n // 2 + 1)
        t = lax.rem(k + d, 16)
        return t // 2, lax.rem(t, 2)

    staged = (
        (rows_ref, rowsv),
        (counts_ref, countsv),
        (x_ref, xv),
        (tiles_ref, own_ts),
        (mask_ref, own_ms),
        (w_ref, wv),
        (og_ref, ogv),
    )

    def start(first, end):
        for i in range(first, end):
            src, dst = staged[i]
            pltpu.make_async_copy(src, dst, in_sem.at[i]).start()

    def arrived(i):
        src, dst = staged[i]
        pltpu.make_async_copy(src, dst, in_sem.at[i]).wait()

    start(0, 3)

    barrier = pltpu.get_barrier_semaphore()

    def greet(where):
        pl.semaphore_signal(barrier, inc=1, device_id=where, device_id_type=MESH)

    def greet_z(n, _):
        greet({"blk": lax.rem(b + 14 - 2 * n, 32)})
        greet({"blk": lax.rem(b + 18 + 2 * n, 32)})
        return 0

    lax.fori_loop(0, 7, greet_z, 0)

    for d in (29, 3, 31, 1):
        greet(at_blk(lax.rem(b + d, 32)))
    greet({"mp": 1 - m})

    def greet_rep(d, _):
        greet({"rep": lax.rem(r + d, 8)})
        return 0

    lax.fori_loop(1, 8, greet_rep, 0)

    iota = functools.partial(lax.broadcasted_iota, jnp.int32)
    expand = (2 * (iota((256, 32), 0) // 16) + h == iota((256, 32), 1)).astype(BF)
    in_slot = lax.rem(iota((256, 16), 0), 16) == iota((256, 16), 1)
    mine = (iota((32, 16), 0) == b).astype(BF)
    arrived(0)
    arrived(1)
    counts = countsv[...].astype(F32).astype(BF)
    sent = dot(mine, counts, ((0,), (0,)))
    row = jnp.where(iota((16, 32), 0).astype(F32) < sent, rowsv[...], 384)
    high = (row // 128).astype(F32).astype(BF)
    low = lax.rem(row, 128).astype(F32).astype(BF)
    full = dot(expand, high, ((1,), (1,))) * 128.0 + dot(expand, low, ((1,), (1,)))
    rowc = jnp.sum(jnp.where(in_slot, full, 0.0), axis=1, keepdims=True)
    pick = (rowc == iota((256, 320), 1).astype(F32)).astype(BF)
    arrived(2)
    outg[...] = dot(pick, xv[...]).astype(BF).reshape(16, 16, 256)

    pl.semaphore_wait(barrier, 26)

    def owner_at(d):
        return lax.rem(2 * lax.rem(z + d, 16) + parity - 4 * r - m + 64, 32) // 2

    def half(p, far):
        i = far if p else 1 - far
        return i, pl.ds(4 * i, 4)

    def deliver(far):
        low, top = F1 + half(0, far)[0], F1 + 2 + half(1, far)[0]

        def one(n, _):
            up = 7 - n
            send(
                outg.at[owner_at(up)],
                fq.at[0, n],
                ss.at[low],
                rs.at[low],
                blk=lax.rem(b + 2 * up, 32),
            )
            send(
                outg.at[owner_at(8 + n)],
                fq.at[1, 7 - n],
                ss.at[top],
                rs.at[top],
                blk=lax.rem(b + 2 * (9 + n), 32),
            )
            return 0

        lax.fori_loop(*((0, 4) if far else (4, 7)), one, 0)

    deliver(0)
    deliver(1)

    send(tiles_ref, mp_tv, key_ss.at[0], key_rs.at[0], mp=1 - m)
    send(mask_ref, mp_mv, key_ss.at[1], key_rs.at[1], mp=1 - m)
    for p in range(2):
        send(
            adj_ref.at[1 - m + 2 * p],
            vall[p].at[pl.ds(5, 5)],
            adj_ss.at[p],
            adj_rs.at[p],
            mp=1 - m,
        )
    fq[0, 7] = outg[owner_at(0)]
    fq[1, 0] = outg[owner_at(15)]

    def first_z(t, j):
        return lax.rem(t // 2 + (9 if j < 2 else 0), 16)

    start(3, 7)

    for p in range(2):
        pltpu.make_async_copy(
            adj_ref.at[m + 2 * p], vall[p].at[pl.ds(0, 5)], loc_sem.at[p]
        ).start()
        vall[p][10] = jnp.zeros((128, 128), BF)

    held = dot(counts, mine)
    expand_r = (iota((512, 32), 0) // 16 == iota((512, 32), 1)).astype(BF)
    in_slot_r = lax.rem(iota((512, 16), 0), 16) == iota((512, 16), 1)
    alive = dot(expand_r, (iota((32, 16), 1).astype(F32) < held).astype(BF))
    live = jnp.sum(jnp.where(in_slot_r, alive, 0.0), axis=1, keepdims=True) > 0.5
    at = iota((32, 512), 1)
    owner = 4 * (at // 64) + 2 * lax.rem(at // 16, 2) + lax.rem(at // 32, 2)
    expand_t = (owner == iota((32, 512), 0)).astype(BF)
    in_slot_t = lax.rem(iota((16, 512), 1), 16) == iota((16, 512), 0)
    full_t = dot(high, expand_t) * 128.0 + dot(low, expand_t)
    rowrv[...] = jnp.sum(jnp.where(in_slot_t, full_t, 0.0), axis=0, keepdims=True)
    pltpu.make_async_copy(rowrv, rowr_ref, out_sem.at[1]).start()

    arrived(3)
    arrived(4)
    drain(mp_tv, key_rs.at[0])
    drain(mp_mv, key_rs.at[1])
    for i, (src, dst) in enumerate(((mp_tv, mp_ts), (mp_mv, mp_ms))):
        pltpu.make_async_copy(src, dst, key_ls.at[i]).start()
    for i, (src, dst) in enumerate(((mp_tv, mp_ts), (mp_mv, mp_ms))):
        pltpu.make_async_copy(src, dst, key_ls.at[i]).wait()

    def build(p):
        j = m + 2 * p
        pltpu.make_async_copy(
            adj_ref.at[m + 2 * p], vall[p].at[pl.ds(0, 5)], loc_sem.at[p]
        ).wait()
        drain(vall[p].at[pl.ds(5, 5)], adj_rs.at[p])

        def places(ts, ms):
            return [
                jnp.where(ms[j, t] == 1, ts[j, 0, t] * 4 + ts[j, 1, t], 16) for t in range(5)
            ]

        own, other = places(own_ts, own_ms), places(mp_ts, mp_ms)
        for row in range(4):
            for col in range(4):
                at = jnp.int32(10)
                for t in range(5):
                    at = jnp.where(own[t] == row * 4 + col, t, at)
                    at = jnp.where(other[t] == row * 4 + col, 5 + t, at)
                tile = vall[p][at]
                dense[p, row * 128:(row + 1) * 128, col * 128:(col + 1) * 128] = tile

    def transpose(p):
        for row in range(4):
            for col in range(4):
                tile = dense[p, row * 128:(row + 1) * 128, col * 128:(col + 1) * 128]
                denset[p, col * 128:(col + 1) * 128, row * 128:(row + 1) * 128] = tile.T

    def others(p):
        for q, to in ((p, 1 - m + 2 * p), (1 - p, 1 - m + 2 * p), (1 - p, m + 2 * p)):
            yield q, to, lax.rem(b - m - 2 * q + to + 32, 32)

    for far in (0, 1):
        for p in range(2):
            drain(fq.at[p, pl.ds(0, 3 + far)], rs.at[F1 + 2 * p + half(p, far)[0]])
        for p in range(2):
            for q, to, t in others(p):
                piece = half(q, far)[1]
                send(
                    fq.at[q, piece],
                    fr.at[p, m + 2 * q, piece],
                    ss.at[XF + q],
                    rs.at[XF + p],
                    **at_blk(t),
                )
    for p in range(2):
        fr[p, m + 2 * p] = fq[p]

    build(0)
    build(1)
    part = None
    for p in range(2):
        drain(fr.at[p, pl.ds(0, 3)], rs.at[XF + p])
        for j in range(4):
            t = lax.rem(b - m - 2 * p + j + 32, 32)
            for n in range(8):
                nat[p, lax.rem(first_z(t, j) + n, 16), lax.rem(t, 2)] = fr[p, j, n]
        term = dot(dense[p], nat[p].reshape(512, 256))
        part = term if part is None else part + term

    r1s[...] = part.astype(BF).reshape(16, 32, 256)

    def scatter(d, _):
        tr, tm = in_group(d)
        send(r1s.at[2 * tr + tm], r1r.at[k], ss.at[R1], rs.at[R1], rep=tr, mp=tm)
        return 0

    lax.fori_loop(0, 15, scatter, 0)
    r1r[k] = r1s[k]
    transpose(0)
    drain(r1r.at[pl.ds(0, 15)], rs.at[R1])
    total = r1r[0].astype(F32)
    for i in range(1, 16):
        total += r1r[i].astype(F32)
    agg[k] = total.astype(BF)

    def gather(d, _):
        tr, tm = in_group(d)
        send(agg.at[k], agg.at[k], ss.at[R2], rs.at[R2], rep=tr, mp=tm)
        return 0

    lax.fori_loop(0, 15, gather, 0)
    transpose(1)
    arrived(5)
    arrived(6)
    drain(agg.at[pl.ds(0, 15)], rs.at[R2])

    for q in range(4):
        rows = slice(q * 128, (q + 1) * 128)
        preact = dot(agg[4 * q:4 * q + 4].reshape(128, 256), wv[...])
        gate = jax.nn.sigmoid(preact)
        hidv[rows, :] = jnp.where(live[rows], preact * gate, 0.0).astype(BF)
        slope = gate * (1.0 + preact * (1.0 - gate))
        pre = jnp.where(live[rows], ogv[rows, :].astype(F32) * slope, 0.0).astype(BF)
        pg[rows, :] = pre
        gb[rows, :] = dot(pre, wv[...], ((1,), (1,))).astype(BF)

    columns = pl.ds(pl.multiple_of((r // 4) * 128, 128), 128)
    wprod[...] = dot(agg[:, :, columns].reshape(512, 128), pg[...], ((0,), (0,))).reshape(8, 16, 256)
    w16 = wprod[lax.rem(r, 4) * 2 + h]
    for a in range(2):
        for c in range(2):
            wa[2 * a + c] = w16[a * 8:(a + 1) * 8, c * 128:(c + 1) * 128]
    war[quad] = wa[quad]
    for e in range(1, 4):
        q = lax.rem(quad + e, 4)
        send(wa.at[q], war.at[quad], ss.at[WA], rs.at[WA], **at_blk(b - quad + q))
    eighth = b // 4

    for p in range(2):
        terms = dot(denset[p], gb[...]).astype(BF).reshape(16, 2, 16, 256)
        for q in range(2):
            pb[p, q, 0:16] = terms[:, q]
            pb[p, q, 16:24] = terms[0:8, q]
        xr[p, m + 2 * p] = pb[p, parity, pl.ds(first_z(b, 2 * p), 8)]

    def share_of(p, far):
        i = half(p, far)[0]
        first, count = ((5 if i else 0), 3) if far else ((3 if i else 0), 5)
        return i, first, pl.ds(first, count)

    def swap_back(far):
        for p in range(2):
            i, first, piece = share_of(p, far)
            for q, to, t in others(p):
                send(
                    pb.at[q, lax.rem(t, 2), pl.ds(first_z(t, 2 * p) + first, piece.size)],
                    xr.at[p, m + 2 * q, piece],
                    ss.at[XS + far],
                    rs.at[XB + 2 * p + i],
                    **at_blk(t),
                )

    swap_back(1)
    pltpu.make_async_copy(hidv, hid_ref, out_sem.at[0]).start()

    drain(war.at[pl.ds(0, 3)], rs.at[WA])
    tile = war[0] + war[1] + war[2] + war[3]
    wb[...] = tile
    wbr[eighth] = tile
    for e in range(1, 8):
        send(wb, wbr.at[eighth], ss.at[WB], rs.at[WB], blk=lax.rem(b + 4 * e, 32))

    drain(xr.at[0, pl.ds(0, 3), pl.ds(0, 6)], ss.at[XS + 1])
    swap_back(0)

    for far in (1, 0):
        for p in range(2):
            i, _, piece = share_of(p, far)
            drain(xr.at[p, pl.ds(0, 3), piece], rs.at[XB + 2 * p + i])
            total = xr[p, 0, piece].astype(F32)
            for n in range(1, 4):
                total += xr[p, n, piece].astype(F32)
            mb[p, piece] = total.astype(BF)
            c = lax.rem(b - 4 * r - m - 2 * p + 64, 32)
            home, slot = c // 4, lax.rem(c, 4) // 2

            def back(n, _):
                away = 7 - n
                send(
                    mb.at[p, n if p == 0 else away],
                    ar.at[slot, r],
                    ss.at[A2S + p],
                    rs.at[A2],
                    blk=lax.rem(b + (32 - 2 * away if p == 0 else 2 * away), 32),
                    rep=home,
                )
                return 0

            lax.fori_loop(*((0, 3) if far else (3, 7)), back, 0)
            if far:
                continue
            here = 7 if p == 0 else 0

            @pl.when(home == r)
            def _():
                pltpu.make_async_copy(mb.at[p, here], ar.at[slot, r], rs.at[A2]).start()

            @pl.when(home != r)
            def _():
                send(mb.at[p, here], ar.at[slot, r], ss.at[SELF + p], rs.at[A2], rep=home)

    drain(wbr.at[pl.ds(0, 7)], rs.at[WB])
    tile = wbr[0]
    for i in range(1, 8):
        tile += wbr[i]
    wc[quad] = tile
    for e in range(1, 4):
        q = lax.rem(quad + e, 4)
        send(wc.at[quad], wc.at[quad], ss.at[WC], rs.at[WC], **at_blk(b - quad + q))

    drain(wc.at[pl.ds(0, 3)], rs.at[WC])
    for a in range(2):
        for c in range(2):
            w_part = wc[2 * a + c]
            wprod[0, a * 8:(a + 1) * 8, c * 128:(c + 1) * 128] = w_part
    wdv[...] = wprod[0].astype(BF)
    pltpu.make_async_copy(wdv, wd_ref.at[kw], rs.at[WD]).start()

    def spread_w(d, _):
        tr, tm = in_group(d)
        send(wdv, wd_ref.at[kw], ss.at[WD], rs.at[WD], rep=tr, mp=tm)
        return 0

    lax.fori_loop(0, 15, spread_w, 0)

    drain(mp_tv, key_ss.at[0])
    drain(mp_mv, key_ss.at[1])
    for p in range(2):
        drain(vall[p].at[pl.ds(5, 5)], adj_ss.at[p])
        for far in (0, 1):
            drain(fq.at[p, pl.ds(0, 3 + far)], ss.at[F1 + 2 * p + half(p, far)[0]])
        drain(fr.at[p, pl.ds(0, 3)], ss.at[XF + p])
    drain(xr.at[pl.ds(0, 2), pl.ds(0, 3), pl.ds(0, 5)], ss.at[XS])
    drain(r1r.at[pl.ds(0, 15)], ss.at[R1])
    drain(agg.at[pl.ds(0, 15)], ss.at[R2])
    drain(wa.at[pl.ds(0, 3)], ss.at[WA])
    drain(wbr.at[pl.ds(0, 7)], ss.at[WB])
    for i, (src, dst) in enumerate(((hidv, hid_ref), (rowrv, rowr_ref))):
        pltpu.make_async_copy(src, dst, out_sem.at[i]).wait()

    drain(ar, rs.at[A2])
    total = ar[:, 0].astype(F32)
    for i in range(1, 8):
        total += ar[:, i].astype(F32)
    gv[...] = total.astype(BF)
    pltpu.make_async_copy(gv, gg_ref.at[kw], rs.at[G]).start()

    def share(d, _):
        tr, tm = in_group(d)
        send(gv, gg_ref.at[kw], ss.at[G], rs.at[G], rep=tr, mp=tm)
        return 0

    lax.fori_loop(0, 15, share, 0)

    drain(wd_ref, rs.at[WD])
    drain(gg_ref, rs.at[G])

    for p in range(2):
        drain(mb.at[p, pl.ds(0, 7)], ss.at[A2S + p])
        c = lax.rem(b - 4 * r - m - 2 * p + 64, 32)

        @pl.when(c // 4 != r)
        def _():
            drain(mb.at[p, 0], ss.at[SELF + p])

    drain(wc.at[pl.ds(0, 3)], ss.at[WC])
    drain(wd_ref.at[pl.ds(0, 15)], ss.at[WD])
    drain(gg_ref.at[pl.ds(0, 15)], ss.at[G])


def finish(hid_in, rowr_in, gg_in, wd_in, hid_ref, wg_ref, ig_ref, hid, rowr, gg, wd, wg, ig, sem):
    incoming = ((rowr_in, rowr), (gg_in, gg), (wd_in, wd), (hid_in, hid))
    outgoing = ((ig, ig_ref), (wg, wg_ref), (hid, hid_ref))
    for i, (src, dst) in enumerate(incoming):
        pltpu.make_async_copy(src, dst, sem.at[i]).start()

    def arrived(i):
        src, dst = incoming[i]
        pltpu.make_async_copy(src, dst, sem.at[i]).wait()

    arrived(0)
    place = (rowr[...] == lax.broadcasted_iota(jnp.int32, (320, 512), 0).astype(F32)).astype(BF)
    arrived(1)
    ig[...] = dot(place, gg[...].reshape(512, 256))
    pltpu.make_async_copy(*outgoing[0], sem.at[4]).start()
    arrived(2)
    wg[...] = wd[...].reshape(256, 256).astype(F32) * (1.0 / 128.0)
    pltpu.make_async_copy(*outgoing[1], sem.at[5]).start()
    arrived(3)
    pltpu.make_async_copy(*outgoing[2], sem.at[6]).start()
    for i, (src, dst) in enumerate(outgoing):
        pltpu.make_async_copy(src, dst, sem.at[4 + i]).wait()


def shards(x_in, weight, out_grad, adj_vals, adj_tiles, adj_mask, send_rows, send_counts):
    hbm = pl.BlockSpec(memory_space=pltpu.HBM)
    V = pltpu.VMEM
    S = pltpu.SMEM
    I32 = jnp.int32
    dma = pltpu.SemaphoreType.DMA
    outs = (
        jax.ShapeDtypeStruct((512, 256), BF),
        jax.ShapeDtypeStruct((256, 256), F32),
        jax.ShapeDtypeStruct((320, 256), F32),
    )
    between = (
        jax.ShapeDtypeStruct((512, 256), BF),
        jax.ShapeDtypeStruct((1, 512), F32),
        jax.ShapeDtypeStruct((16, 2, 16, 256), BF),
        jax.ShapeDtypeStruct((16, 16, 256), BF),
    )
    results = pl.pallas_call(
        kernel,
        out_shape=between,
        in_specs=[hbm] * 8,
        out_specs=(hbm,) * 4,
        scratch_shapes=[V((11, 128, 128), BF)] * 2
        + [
            V((320, 256), BF),
            V((256, 256), BF),
            V((512, 256), BF),
            V((16, 32), I32),
            V((32, 32), I32),
            S((4, 2, 5), I32),
            S((4, 5), I32),
            V((4, 2, 5), I32),
            V((4, 5), I32),
            S((4, 2, 5), I32),
            S((4, 5), I32),
            V((2, 512, 512), BF),
            V((2, 512, 512), BF),
            V((16, 16, 256), BF),
            V((2, 8, 16, 256), BF),
            V((2, 4, 8, 16, 256), BF),
            V((2, 16, 2, 16, 256), BF),
            V((16, 32, 256), BF),
            V((16, 32, 256), BF),
            V((16, 32, 256), BF),
            V((512, 256), BF),
            V((512, 256), BF),
            V((2, 2, 24, 16, 256), BF),
            V((2, 4, 8, 16, 256), BF),
            V((2, 8, 16, 256), BF),
            V((2, 8, 16, 256), BF),
            V((2, 16, 256), BF),
            V((8, 16, 256), F32),
            V((4, 8, 128), F32),
            V((4, 8, 128), F32),
            V((8, 128), F32),
            V((8, 8, 128), F32),
            V((4, 8, 128), F32),
            V((16, 256), BF),
            V((512, 256), BF),
            V((1, 512), F32),
            dma((2,)),
            dma((7,)),
            dma((2,)),
            dma((2,)),
            dma((2,)),
            dma((2,)),
            dma((2,)),
            dma((2,)),
            dma((24,)),
            dma((24,)),
        ],
        compiler_params=pltpu.CompilerParams(
            collective_id=0, has_side_effects=True, vmem_limit_bytes=62 * 1024 * 1024
        ),
        name="graph_layer",
    )(
        jnp.swapaxes(adj_tiles[0], 1, 2),
        adj_mask[0],
        x_in,
        weight,
        out_grad,
        send_rows[0].T,
        send_counts,
        adj_vals[0],
    )
    return pl.pallas_call(
        finish,
        out_shape=outs,
        in_specs=[hbm] * 4,
        out_specs=(hbm,) * 3,
        scratch_shapes=[V(o.shape, o.dtype) for o in between + outs[1:]] + [dma((7,))],
        compiler_params=pltpu.CompilerParams(vmem_limit_bytes=62 * 1024 * 1024),
        name="finish",
    )(*results)


def solution(mesh):
    placed = (
        P("blk", None),
        P(),
        P("blk", None),
        P("blk", "rep", "mp", None, None),
        P("blk", "rep", "mp", None),
        P("blk", "rep", "mp"),
        P("blk", None, None),
        P(),
    )
    return jax.shard_map(
        shards,
        mesh=mesh,
        in_specs=placed,
        out_specs=(P("blk", None), P(), P("blk", None)),
        check_vma=False,
    )
```

```python
import functools

import jax
import jax.numpy as jnp
from jax import lax
from jax.experimental import pallas as pl
from jax.experimental.pallas import tpu as pltpu
from jax.sharding import PartitionSpec as P

MESH = pl.DeviceIdType.MESH
BF = jnp.bfloat16
F32 = jnp.float32


def dot(a, b, dims=((1,), (0,))):
    return lax.dot_general(a, b, (dims, ((), ())), preferred_element_type=F32)


def send(src, dst, ssem, rsem, **where):
    pltpu.make_async_remote_copy(
        src_ref=src,
        dst_ref=dst,
        send_sem=ssem,
        recv_sem=rsem,
        device_id=where,
        device_id_type=MESH,
    ).start()


def drain(ref, sem):
    pltpu.make_async_copy(ref, ref, sem).wait()


def kernel(
    tiles_ref,
    mask_ref,
    x_ref,
    w_ref,
    og_ref,
    rows_ref,
    counts_ref,
    adj_ref,
    hid_ref,
    rowr_ref,
    gg_ref,
    wd_ref,
    v0, v1,
    xv, wv, ogv, rowsv, countsv,
    own_ts, own_ms, mp_tv, mp_mv, mp_ts, mp_ms,
    dense, denset,
    outg, fq, fr, nat,
    r1s, r1r, agg,
    pg, gb,
    pb, xr, mb, ar, gv,
    wprod, wa, war, wb, wbr, wc, wdv,
    hidv, rowrv,
    loc_sem, in_sem, out_sem, adj_ss, adj_rs, key_ss, key_rs, key_ls,
    ss, rs,
):
    vall = (v0, v1)
    b = lax.axis_index("blk")
    r = lax.axis_index("rep")
    m = lax.axis_index("mp")
    z = b // 2
    parity = lax.rem(b, 2)
    h = lax.rem(m + b, 2)
    k = r * 2 + m
    kw = r * 2 + h
    quad = lax.rem(b, 4)
    R1, R2, G, WA, WB, WC, WD, A2 = range(8)
    XF, XS, A2S, SELF, F1, XB = 8, 10, 12, 14, 16, 20

    def at_blk(t):
        return {"blk": t, "mp": lax.rem(h + t, 2)}

    def in_group(n):
        d = 8 + jnp.where(lax.rem(n, 2) == 0, -(n // 2), n // 2 + 1)
        t = lax.rem(k + d, 16)
        return t // 2, lax.rem(t, 2)

    staged = (
        (rows_ref, rowsv),
        (counts_ref, countsv),
        (x_ref, xv),
        (tiles_ref, own_ts),
        (mask_ref, own_ms),
        (w_ref, wv),
        (og_ref, ogv),
    )

    def start(first, end):
        for i in range(first, end):
            src, dst = staged[i]
            pltpu.make_async_copy(src, dst, in_sem.at[i]).start()

    def arrived(i):
        src, dst = staged[i]
        pltpu.make_async_copy(src, dst, in_sem.at[i]).wait()

    start(0, 3)

    barrier = pltpu.get_barrier_semaphore()

    def greet(where):
        pl.semaphore_signal(barrier, inc=1, device_id=where, device_id_type=MESH)

    def greet_z(n, _):
        greet({"blk": lax.rem(b + 14 - 2 * n, 32)})
        greet({"blk": lax.rem(b + 18 + 2 * n, 32)})
        return 0

    lax.fori_loop(0, 7, greet_z, 0)

    for d in (29, 3, 31, 1):
        greet(at_blk(lax.rem(b + d, 32)))
    greet({"mp": 1 - m})

    def greet_rep(d, _):
        greet({"rep": lax.rem(r + d, 8)})
        return 0

    lax.fori_loop(1, 8, greet_rep, 0)

    iota = functools.partial(lax.broadcasted_iota, jnp.int32)
    expand = (2 * (iota((256, 32), 0) // 16) + h == iota((256, 32), 1)).astype(BF)
    in_slot = lax.rem(iota((256, 16), 0), 16) == iota((256, 16), 1)
    mine = (iota((32, 16), 0) == b).astype(BF)
    arrived(0)
    arrived(1)
    counts = countsv[...].astype(F32).astype(BF)
    sent = dot(mine, counts, ((0,), (0,)))
    row = jnp.where(iota((16, 32), 0).astype(F32) < sent, rowsv[...], 384)
    high = (row // 128).astype(F32).astype(BF)
    low = lax.rem(row, 128).astype(F32).astype(BF)
    full = dot(expand, high, ((1,), (1,))) * 128.0 + dot(expand, low, ((1,), (1,)))
    rowc = jnp.sum(jnp.where(in_slot, full, 0.0), axis=1, keepdims=True)
    pick = (rowc == iota((256, 320), 1).astype(F32)).astype(BF)
    arrived(2)
    outg[...] = dot(pick, xv[...]).astype(BF).reshape(16, 16, 256)

    pl.semaphore_wait(barrier, 26)

    def owner_at(d):
        return lax.rem(2 * lax.rem(z + d, 16) + parity - 4 * r - m + 64, 32) // 2

    def half(p, far):
        i = far if p else 1 - far
        return i, pl.ds(4 * i, 4)

    def deliver(far):
        low, top = F1 + half(0, far)[0], F1 + 2 + half(1, far)[0]

        def one(n, _):
            up = 7 - n
            send(
                outg.at[owner_at(up)],
                fq.at[0, n],
                ss.at[low],
                rs.at[low],
                blk=lax.rem(b + 2 * up, 32),
            )
            send(
                outg.at[owner_at(8 + n)],
                fq.at[1, 7 - n],
                ss.at[top],
                rs.at[top],
                blk=lax.rem(b + 2 * (9 + n), 32),
            )
            return 0

        lax.fori_loop(*((0, 4) if far else (4, 7)), one, 0)

    deliver(0)
    deliver(1)

    send(tiles_ref, mp_tv, key_ss.at[0], key_rs.at[0], mp=1 - m)
    send(mask_ref, mp_mv, key_ss.at[1], key_rs.at[1], mp=1 - m)
    for p in range(2):
        send(
            adj_ref.at[1 - m + 2 * p],
            vall[p].at[pl.ds(5, 5)],
            adj_ss.at[p],
            adj_rs.at[p],
            mp=1 - m,
        )
    fq[0, 7] = outg[owner_at(0)]
    fq[1, 0] = outg[owner_at(15)]

    def first_z(t, j):
        return lax.rem(t // 2 + (9 if j < 2 else 0), 16)

    start(3, 7)

    for p in range(2):
        pltpu.make_async_copy(
            adj_ref.at[m + 2 * p], vall[p].at[pl.ds(0, 5)], loc_sem.at[p]
        ).start()
        vall[p][10] = jnp.zeros((128, 128), BF)

    held = dot(counts, mine)
    expand_r = (iota((512, 32), 0) // 16 == iota((512, 32), 1)).astype(BF)
    in_slot_r = lax.rem(iota((512, 16), 0), 16) == iota((512, 16), 1)
    alive = dot(expand_r, (iota((32, 16), 1).astype(F32) < held).astype(BF))
    live = jnp.sum(jnp.where(in_slot_r, alive, 0.0), axis=1, keepdims=True) > 0.5
    at = iota((32, 512), 1)
    owner = 4 * (at // 64) + 2 * lax.rem(at // 16, 2) + lax.rem(at // 32, 2)
    expand_t = (owner == iota((32, 512), 0)).astype(BF)
    in_slot_t = lax.rem(iota((16, 512), 1), 16) == iota((16, 512), 0)
    full_t = dot(high, expand_t) * 128.0 + dot(low, expand_t)
    rowrv[...] = jnp.sum(jnp.where(in_slot_t, full_t, 0.0), axis=0, keepdims=True)
    pltpu.make_async_copy(rowrv, rowr_ref, out_sem.at[1]).start()

    arrived(3)
    arrived(4)
    drain(mp_tv, key_rs.at[0])
    drain(mp_mv, key_rs.at[1])
    for i, (src, dst) in enumerate(((mp_tv, mp_ts), (mp_mv, mp_ms))):
        pltpu.make_async_copy(src, dst, key_ls.at[i]).start()
    for i, (src, dst) in enumerate(((mp_tv, mp_ts), (mp_mv, mp_ms))):
        pltpu.make_async_copy(src, dst, key_ls.at[i]).wait()

    def build(p):
        j = m + 2 * p
        pltpu.make_async_copy(
            adj_ref.at[m + 2 * p], vall[p].at[pl.ds(0, 5)], loc_sem.at[p]
        ).wait()
        drain(vall[p].at[pl.ds(5, 5)], adj_rs.at[p])

        def places(ts, ms):
            return [
                jnp.where(ms[j, t] == 1, ts[j, 0, t] * 4 + ts[j, 1, t], 16) for t in range(5)
            ]

        own, other = places(own_ts, own_ms), places(mp_ts, mp_ms)
        for row in range(4):
            for col in range(4):
                at = jnp.int32(10)
                for t in range(5):
                    at = jnp.where(own[t] == row * 4 + col, t, at)
                    at = jnp.where(other[t] == row * 4 + col, 5 + t, at)
                tile = vall[p][at]
                dense[p, row * 128:(row + 1) * 128, col * 128:(col + 1) * 128] = tile

    def transpose(p):
        for row in range(4):
            for col in range(4):
                tile = dense[p, row * 128:(row + 1) * 128, col * 128:(col + 1) * 128]
                denset[p, col * 128:(col + 1) * 128, row * 128:(row + 1) * 128] = tile.T

    def others(p):
        for q, to in ((p, 1 - m + 2 * p), (1 - p, 1 - m + 2 * p), (1 - p, m + 2 * p)):
            yield q, to, lax.rem(b - m - 2 * q + to + 32, 32)

    for far in (0, 1):
        for p in range(2):
            drain(fq.at[p, pl.ds(0, 3 + far)], rs.at[F1 + 2 * p + half(p, far)[0]])
        for p in range(2):
            for q, to, t in others(p):
                piece = half(q, far)[1]
                send(
                    fq.at[q, piece],
                    fr.at[p, m + 2 * q, piece],
                    ss.at[XF + q],
                    rs.at[XF + p],
                    **at_blk(t),
                )
    for p in range(2):
        fr[p, m + 2 * p] = fq[p]

    build(0)
    build(1)
    part = None
    for p in range(2):
        drain(fr.at[p, pl.ds(0, 3)], rs.at[XF + p])
        for j in range(4):
            t = lax.rem(b - m - 2 * p + j + 32, 32)
            for n in range(8):
                nat[p, lax.rem(first_z(t, j) + n, 16), lax.rem(t, 2)] = fr[p, j, n]
        term = dot(dense[p], nat[p].reshape(512, 256))
        part = term if part is None else part + term

    r1s[...] = part.astype(BF).reshape(16, 32, 256)

    def scatter(d, _):
        tr, tm = in_group(d)
        send(r1s.at[2 * tr + tm], r1r.at[k], ss.at[R1], rs.at[R1], rep=tr, mp=tm)
        return 0

    lax.fori_loop(0, 15, scatter, 0)
    r1r[k] = r1s[k]
    transpose(0)
    drain(r1r.at[pl.ds(0, 15)], rs.at[R1])
    total = r1r[0].astype(F32)
    for i in range(1, 16):
        total += r1r[i].astype(F32)
    agg[k] = total.astype(BF)

    def gather(d, _):
        tr, tm = in_group(d)
        send(agg.at[k], agg.at[k], ss.at[R2], rs.at[R2], rep=tr, mp=tm)
        return 0

    lax.fori_loop(0, 15, gather, 0)
    transpose(1)
    arrived(5)
    arrived(6)
    drain(agg.at[pl.ds(0, 15)], rs.at[R2])

    for q in range(4):
        rows = slice(q * 128, (q + 1) * 128)
        preact = dot(agg[4 * q:4 * q + 4].reshape(128, 256), wv[...])
        gate = jax.nn.sigmoid(preact)
        hidv[rows, :] = jnp.where(live[rows], preact * gate, 0.0).astype(BF)
        slope = gate * (1.0 + preact * (1.0 - gate))
        pre = jnp.where(live[rows], ogv[rows, :].astype(F32) * slope, 0.0).astype(BF)
        pg[rows, :] = pre
        gb[rows, :] = dot(pre, wv[...], ((1,), (1,))).astype(BF)

    columns = pl.ds(pl.multiple_of((r // 4) * 128, 128), 128)
    wprod[...] = dot(agg[:, :, columns].reshape(512, 128), pg[...], ((0,), (0,))).reshape(8, 16, 256)
    w16 = wprod[lax.rem(r, 4) * 2 + h]
    for a in range(2):
        for c in range(2):
            wa[2 * a + c] = w16[a * 8:(a + 1) * 8, c * 128:(c + 1) * 128]
    war[quad] = wa[quad]
    for e in range(1, 4):
        q = lax.rem(quad + e, 4)
        send(wa.at[q], war.at[quad], ss.at[WA], rs.at[WA], **at_blk(b - quad + q))
    eighth = b // 4

    for p in range(2):
        terms = dot(denset[p], gb[...]).astype(BF).reshape(16, 2, 16, 256)
        for q in range(2):
            pb[p, q, 0:16] = terms[:, q]
            pb[p, q, 16:24] = terms[0:8, q]
        xr[p, m + 2 * p] = pb[p, parity, pl.ds(first_z(b, 2 * p), 8)]

    def share_of(p, far):
        i = half(p, far)[0]
        first, count = ((5 if i else 0), 3) if far else ((3 if i else 0), 5)
        return i, first, pl.ds(first, count)

    def swap_back(far):
        for p in range(2):
            i, first, piece = share_of(p, far)
            for q, to, t in others(p):
                send(
                    pb.at[q, lax.rem(t, 2), pl.ds(first_z(t, 2 * p) + first, piece.size)],
                    xr.at[p, m + 2 * q, piece],
                    ss.at[XS + far],
                    rs.at[XB + 2 * p + i],
                    **at_blk(t),
                )

    swap_back(1)
    pltpu.make_async_copy(hidv, hid_ref, out_sem.at[0]).start()

    drain(war.at[pl.ds(0, 3)], rs.at[WA])
    tile = war[0] + war[1] + war[2] + war[3]
    wb[...] = tile
    wbr[eighth] = tile
    for e in range(1, 8):
        send(wb, wbr.at[eighth], ss.at[WB], rs.at[WB], blk=lax.rem(b + 4 * e, 32))

    drain(xr.at[0, pl.ds(0, 3), pl.ds(0, 6)], ss.at[XS + 1])
    swap_back(0)

    for far in (1, 0):
        for p in range(2):
            i, _, piece = share_of(p, far)
            drain(xr.at[p, pl.ds(0, 3), piece], rs.at[XB + 2 * p + i])
            total = xr[p, 0, piece].astype(F32)
            for n in range(1, 4):
                total += xr[p, n, piece].astype(F32)
            mb[p, piece] = total.astype(BF)
            c = lax.rem(b - 4 * r - m - 2 * p + 64, 32)
            home, slot = c // 4, lax.rem(c, 4) // 2

            def back(n, _):
                away = 7 - n
                send(
                    mb.at[p, n if p == 0 else away],
                    ar.at[slot, r],
                    ss.at[A2S + p],
                    rs.at[A2],
                    blk=lax.rem(b + (32 - 2 * away if p == 0 else 2 * away), 32),
                    rep=home,
                )
                return 0

            lax.fori_loop(*((0, 3) if far else (3, 7)), back, 0)
            if far:
                continue
            here = 7 if p == 0 else 0

            @pl.when(home == r)
            def _():
                pltpu.make_async_copy(mb.at[p, here], ar.at[slot, r], rs.at[A2]).start()

            @pl.when(home != r)
            def _():
                send(mb.at[p, here], ar.at[slot, r], ss.at[SELF + p], rs.at[A2], rep=home)

    drain(wbr.at[pl.ds(0, 7)], rs.at[WB])
    tile = wbr[0]
    for i in range(1, 8):
        tile += wbr[i]
    wc[quad] = tile
    for e in range(1, 4):
        q = lax.rem(quad + e, 4)
        send(wc.at[quad], wc.at[quad], ss.at[WC], rs.at[WC], **at_blk(b - quad + q))

    drain(wc.at[pl.ds(0, 3)], rs.at[WC])
    for a in range(2):
        for c in range(2):
            w_part = wc[2 * a + c]
            wprod[0, a * 8:(a + 1) * 8, c * 128:(c + 1) * 128] = w_part
    wdv[...] = wprod[0].astype(BF)
    pltpu.make_async_copy(wdv, wd_ref.at[kw], rs.at[WD]).start()

    def spread_w(d, _):
        tr, tm = in_group(d)
        send(wdv, wd_ref.at[kw], ss.at[WD], rs.at[WD], rep=tr, mp=tm)
        return 0

    lax.fori_loop(0, 15, spread_w, 0)

    drain(mp_tv, key_ss.at[0])
    drain(mp_mv, key_ss.at[1])
    for p in range(2):
        drain(vall[p].at[pl.ds(5, 5)], adj_ss.at[p])
        for far in (0, 1):
            drain(fq.at[p, pl.ds(0, 3 + far)], ss.at[F1 + 2 * p + half(p, far)[0]])
        drain(fr.at[p, pl.ds(0, 3)], ss.at[XF + p])
    drain(xr.at[pl.ds(0, 2), pl.ds(0, 3), pl.ds(0, 5)], ss.at[XS])
    drain(r1r.at[pl.ds(0, 15)], ss.at[R1])
    drain(agg.at[pl.ds(0, 15)], ss.at[R2])
    drain(wa.at[pl.ds(0, 3)], ss.at[WA])
    drain(wbr.at[pl.ds(0, 7)], ss.at[WB])
    for i, (src, dst) in enumerate(((hidv, hid_ref), (rowrv, rowr_ref))):
        pltpu.make_async_copy(src, dst, out_sem.at[i]).wait()

    drain(ar, rs.at[A2])
    total = ar[:, 0].astype(F32)
    for i in range(1, 8):
        total += ar[:, i].astype(F32)
    gv[...] = total.astype(BF)
    pltpu.make_async_copy(gv, gg_ref.at[kw], rs.at[G]).start()

    def share(d, _):
        tr, tm = in_group(d)
        send(gv, gg_ref.at[kw], ss.at[G], rs.at[G], rep=tr, mp=tm)
        return 0

    lax.fori_loop(0, 15, share, 0)

    drain(wd_ref, rs.at[WD])
    drain(gg_ref, rs.at[G])

    for p in range(2):
        drain(mb.at[p, pl.ds(0, 7)], ss.at[A2S + p])
        c = lax.rem(b - 4 * r - m - 2 * p + 64, 32)

        @pl.when(c // 4 != r)
        def _():
            drain(mb.at[p, 0], ss.at[SELF + p])

    drain(wc.at[pl.ds(0, 3)], ss.at[WC])
    drain(wd_ref.at[pl.ds(0, 15)], ss.at[WD])
    drain(gg_ref.at[pl.ds(0, 15)], ss.at[G])


def finish(hid_in, rowr_in, gg_in, wd_in, hid_ref, wg_ref, ig_ref, hid, rowr, gg, wd, wg, ig, sem):
    incoming = ((rowr_in, rowr), (gg_in, gg), (wd_in, wd), (hid_in, hid))
    outgoing = ((ig, ig_ref), (wg, wg_ref), (hid, hid_ref))
    for i, (src, dst) in enumerate(incoming):
        pltpu.make_async_copy(src, dst, sem.at[i]).start()

    def arrived(i):
        src, dst = incoming[i]
        pltpu.make_async_copy(src, dst, sem.at[i]).wait()

    arrived(0)
    place = (rowr[...] == lax.broadcasted_iota(jnp.int32, (320, 512), 0).astype(F32)).astype(BF)
    arrived(3)
    pltpu.make_async_copy(*outgoing[2], sem.at[6]).start()
    arrived(1)
    ig[...] = dot(place, gg[...].reshape(512, 256))
    pltpu.make_async_copy(*outgoing[0], sem.at[4]).start()
    arrived(2)
    wg[...] = wd[...].reshape(256, 256).astype(F32) * (1.0 / 128.0)
    pltpu.make_async_copy(*outgoing[1], sem.at[5]).start()
    for i, (src, dst) in enumerate(outgoing):
        pltpu.make_async_copy(src, dst, sem.at[4 + i]).wait()


def shards(x_in, weight, out_grad, adj_vals, adj_tiles, adj_mask, send_rows, send_counts):
    hbm = pl.BlockSpec(memory_space=pltpu.HBM)
    V = pltpu.VMEM
    S = pltpu.SMEM
    I32 = jnp.int32
    dma = pltpu.SemaphoreType.DMA
    outs = (
        jax.ShapeDtypeStruct((512, 256), BF),
        jax.ShapeDtypeStruct((256, 256), F32),
        jax.ShapeDtypeStruct((320, 256), F32),
    )
    between = (
        jax.ShapeDtypeStruct((512, 256), BF),
        jax.ShapeDtypeStruct((1, 512), F32),
        jax.ShapeDtypeStruct((16, 2, 16, 256), BF),
        jax.ShapeDtypeStruct((16, 16, 256), BF),
    )
    results = pl.pallas_call(
        kernel,
        out_shape=between,
        in_specs=[hbm] * 8,
        out_specs=(hbm,) * 4,
        scratch_shapes=[V((11, 128, 128), BF)] * 2
        + [
            V((320, 256), BF),
            V((256, 256), BF),
            V((512, 256), BF),
            V((16, 32), I32),
            V((32, 32), I32),
            S((4, 2, 5), I32),
            S((4, 5), I32),
            V((4, 2, 5), I32),
            V((4, 5), I32),
            S((4, 2, 5), I32),
            S((4, 5), I32),
            V((2, 512, 512), BF),
            V((2, 512, 512), BF),
            V((16, 16, 256), BF),
            V((2, 8, 16, 256), BF),
            V((2, 4, 8, 16, 256), BF),
            V((2, 16, 2, 16, 256), BF),
            V((16, 32, 256), BF),
            V((16, 32, 256), BF),
            V((16, 32, 256), BF),
            V((512, 256), BF),
            V((512, 256), BF),
            V((2, 2, 24, 16, 256), BF),
            V((2, 4, 8, 16, 256), BF),
            V((2, 8, 16, 256), BF),
            V((2, 8, 16, 256), BF),
            V((2, 16, 256), BF),
            V((8, 16, 256), F32),
            V((4, 8, 128), F32),
            V((4, 8, 128), F32),
            V((8, 128), F32),
            V((8, 8, 128), F32),
            V((4, 8, 128), F32),
            V((16, 256), BF),
            V((512, 256), BF),
            V((1, 512), F32),
            dma((2,)),
            dma((7,)),
            dma((2,)),
            dma((2,)),
            dma((2,)),
            dma((2,)),
            dma((2,)),
            dma((2,)),
            dma((24,)),
            dma((24,)),
        ],
        compiler_params=pltpu.CompilerParams(
            collective_id=0, has_side_effects=True, vmem_limit_bytes=62 * 1024 * 1024
        ),
        name="graph_layer",
    )(
        jnp.swapaxes(adj_tiles[0], 1, 2),
        adj_mask[0],
        x_in,
        weight,
        out_grad,
        send_rows[0].T,
        send_counts,
        adj_vals[0],
    )
    return pl.pallas_call(
        finish,
        out_shape=outs,
        in_specs=[hbm] * 4,
        out_specs=(hbm,) * 3,
        scratch_shapes=[V(o.shape, o.dtype) for o in between + outs[1:]] + [dma((7,))],
        compiler_params=pltpu.CompilerParams(vmem_limit_bytes=62 * 1024 * 1024),
        name="finish",
    )(*results)


def solution(mesh):
    placed = (
        P("blk", None),
        P(),
        P("blk", None),
        P("blk", "rep", "mp", None, None),
        P("blk", "rep", "mp", None),
        P("blk", "rep", "mp"),
        P("blk", None, None),
        P(),
    )
    return jax.shard_map(
        shards,
        mesh=mesh,
        in_specs=placed,
        out_specs=(P("blk", None), P(), P("blk", None)),
        check_vma=False,
    )
```
